256 devices in a mesh: tm: 32 (over y, z_hi, core), head: 8 (over z_lo, x).
Axes of the slice: x: 4, y: 4, z: 8 (z_hi: 4, z_lo: 2; z = z_hi * 2 + z_lo), core: 2. Of those that a mesh axis runs over, the one named last changes fastest.
Arguments:
- tokens: bfloat16 [8192, 3072], P('tm', 'head'), may hold values from -14 to 14
- qkv_weight: bfloat16 [3, 3072, 3072], P(None, None, 'head'), may hold values from -0.109375 to 0.109375
- out_weight: bfloat16 [3072, 3072], P('head'), may hold values from -0.109375 to 0.109375
- segment_ids: int32 [8192], replicated, may hold values from 0 to 2, never falling along the last dimension, each value on 1 to 4096 neighbouring positions
- inner_w1: float32 [48, 64, 256], P('head'), may hold values from -0.75 to 0.75
- inner_b1: float32 [48, 256], P('head'), may hold values from -3 to 3
- inner_w2: float32 [48, 256, 64], P('head'), may hold values from -0.375 to 0.375
- inner_b2: float32 [48, 64], P('head'), may hold values from -3 to 3
- norm_gain: float32 [48, 64], P('head'), may hold values from 0.1 to 1.9
- norm_bias: float32 [48, 64], P('head'), may hold values from -2 to 2
- inner_rate: float32 [48], P('head'), may hold values from 0.1 to 1
- out_gate: float32 [48, 64], P('head'), may hold values from -3 to 3
Outputs:
- layer_out: bfloat16 [8192, 3072], P('tm', 'head')
The draws below stay inside these ranges and needn't reach their ends.
Inputs may be any that keep to these rules, and one draw needn't show every extreme that they name: `segment_ids`: segment ids never fall along the tokens; each segment has 1 to 4096 tokens and one has exactly 4096.
All inputs are finite; a program needn't handle non-finite values.
Results may differ from the reference program's by a relative error of at most 0.019.
The reference program's roundings to bfloat16 on the way (of `weights` and `mixed`) count: a program that leaves them out, or rounds other values in their place, can miss the bound.
Values may be sent and summed in bfloat16 or wider, within the bound.
A program may use at most 128 MiB of HBM per device.

```python
import math
import jax
import jax.numpy as jnp
import numpy as np
from jax import lax

D = 3072
HEADS = 48
HDIM = 64
HID = 256
GROUP = 64
TOKENS = 8192
SEG_MOST = 4096
INNER = 3072


def draw_tokens(key, part):
    key = jax.random.fold_in(key, 11)
    first = jax.random.fold_in(key, 0)
    base = jnp.clip(jax.random.normal(first, (TOKENS, D), jnp.float32), -5.0, 5.0)
    return base.astype(jnp.bfloat16)


def levels(own_key, shape, cuts, least, largest):
    level, own = 1.0, jax.random.fold_in(own_key, 6)
    for dim, shards_of in cuts:
        draws = jnp.exp(jax.random.uniform(jax.random.fold_in(own, dim), (shards_of,), jnp.float32, least / len(cuts), largest / len(cuts)))
        level = level * jnp.repeat(draws, shape[dim] // shards_of).reshape([-1 if axis == dim else 1 for axis in range(len(shape))])
    return level


def split_up(amount, total, most, skew):
    loads = [(1 << 20) // math.isqrt(standing ** skew) + 1 for standing in range(2, amount + 1)]
    rest, counts = total - most - (amount - 1), [1] * (amount - 1)
    while rest > 0:
        movable = [i for i in range(amount - 1) if counts[i] < most]
        whole, remaining = sum([loads[i] for i in movable]), rest
        for i in movable:
            addition = min(most - counts[i], max(1, remaining * loads[i] // whole), rest)
            counts[i] = counts[i] + addition
            rest = rest - addition
    return np.array([most] + counts)


def uneven_parts(key, count, total, bound, slope):
    if count == 2:
        one = jax.random.randint(key, (), max(1, total - bound), min(bound, total - 1) + 1)
        return jnp.stack([one, total - one])
    lengths = jnp.asarray(split_up(count, total, bound, slope), jnp.int32)
    pairs = (count - 1) // 2
    donor, sink = lengths[1:1 + 2 * pairs:2], lengths[2:2 + 2 * pairs:2]
    margin = jnp.minimum(donor - 1, bound - sink)
    passed = jax.random.randint(jax.random.fold_in(key, 1), (pairs,), 0, 1 << 20) % (margin + 1)
    lengths = lengths.at[1:1 + 2 * pairs:2].set(donor - passed).at[2:2 + 2 * pairs:2].set(sink + passed)
    return lengths[jax.random.permutation(jax.random.fold_in(key, 2), count)]


def normal_values(rng, extent, scale, bound, cuts=(), held_as=jnp.bfloat16):
    entries = jax.random.normal(rng, extent, jnp.float32) * scale
    if len(cuts) > 0:
        entries = levels(rng, extent, cuts, -0.22, 0.18) * entries
    return jnp.clip(entries, min=-bound, max=bound).astype(held_as)


def setup_inputs(seed: int = 0) -> dict:
    seeds = jax.random.split(jax.random.key(seed), 13)
    return {
        "tokens": draw_tokens(jax.random.fold_in(seeds[12], 71), 0),
        "qkv_weight": normal_values(seeds[1], (3, D, INNER), D ** -0.5, 0.109375, ((2, 8),)),
        "out_weight": normal_values(seeds[2], (INNER, D), INNER ** -0.5, 0.109375, ((0, 8),)),
        "segment_ids": jnp.searchsorted(jnp.cumsum(uneven_parts(seeds[3], 3, TOKENS, SEG_MOST, 2)), jnp.arange(TOKENS), side="right").astype(jnp.int32),
        "inner_w1": normal_values(seeds[4], (HEADS, HDIM, HID), HDIM ** -0.5, 0.75, ((0, 8),), jnp.float32),
        "inner_b1": normal_values(seeds[5], (HEADS, HID), 0.5, 3.0, ((0, 8),), jnp.float32),
        "inner_w2": normal_values(seeds[6], (HEADS, HID, HDIM), HID ** -0.5, 0.375, ((0, 8),), jnp.float32),
        "inner_b2": normal_values(seeds[7], (HEADS, HDIM), 0.5, 3.0, ((0, 8),), jnp.float32),
        "norm_gain": jnp.clip(1.0 + 0.18 * jax.random.normal(seeds[8], (HEADS, HDIM), jnp.float32), 0.1, 1.9),
        "norm_bias": normal_values(seeds[9], (HEADS, HDIM), 0.3, 2.0, ((0, 8),), jnp.float32),
        "inner_rate": jnp.clip(jnp.exp(math.log(1.0) - 2.3025851 * jax.random.uniform(seeds[10], (HEADS,), jnp.float32) ** levels(seeds[10], (HEADS,), ((0, 8),), -0.2, 0.2)), 0.1, 1.0),
        "out_gate": normal_values(seeds[11], (HEADS, HDIM), 1.0, 3.0, ((0, 8),), jnp.float32),
    }


EPS = 1e-06
HIGH = lax.Precision.HIGHEST

def smooth_gate(value_in):
    return jax.nn.gelu(value_in, approximate=True)

def rms_scaled(field):
    return field * lax.rsqrt(lax.optimization_barrier(jnp.mean(field * field, -1, keepdims=True)) + EPS)

def layer_normed(field, norm_gain, norm_bias):
    center = field - lax.optimization_barrier(jnp.mean(field, -1, keepdims=True))
    inverse = lax.rsqrt(lax.optimization_barrier(jnp.mean(center * center, -1, keepdims=True)) + EPS)
    normed = center * inverse
    return (normed, inverse, normed * norm_gain + norm_bias)

def inner_step(inner_state, pieces, head_consts):
    w_first, b_first, w_second, b_second = inner_state
    key_rows, value_rows, query_rows = pieces
    norm_gain, norm_bias, step_rate = head_consts
    hidden = jnp.dot(key_rows, w_first, precision=HIGH) + b_first
    active, gelu_back = jax.vjp(smooth_gate, hidden)
    recon = jnp.dot(active, w_second, precision=HIGH) + b_second
    normed, inverse, produced = layer_normed(recon, norm_gain, norm_bias)
    grad_norm = (produced - (value_rows - key_rows)) * norm_gain
    grad_recon = inverse * (grad_norm - lax.optimization_barrier(jnp.mean(grad_norm, -1, keepdims=True)) - normed * lax.optimization_barrier(jnp.mean(grad_norm * normed, -1, keepdims=True)))
    grad_active = jnp.dot(grad_recon, w_second.T, precision=HIGH)
    grad_hidden = gelu_back(grad_active)[0]
    step_size = step_rate / (key_rows.shape[0] * key_rows.shape[1])
    w_first = w_first - step_size * jnp.dot(key_rows.T, grad_hidden, precision=HIGH)
    b_first = b_first - step_size * lax.optimization_barrier(jnp.sum(grad_hidden, 0))
    w_second = w_second - step_size * jnp.dot(active.T, grad_recon, precision=HIGH)
    b_second = b_second - step_size * lax.optimization_barrier(jnp.sum(grad_recon, 0))
    query_hidden = smooth_gate(jnp.dot(query_rows, w_first, precision=HIGH) + b_first)
    query_recon = jnp.dot(query_hidden, w_second, precision=HIGH) + b_second
    result = query_rows + layer_normed(query_recon, norm_gain, norm_bias)[2]
    return ((w_first, b_first, w_second, b_second), result)

def sweep_heads(init_params, key_rows, value_rows, query_rows, consts):

    def one_head(start_state, head_keys, head_values, head_queries, head_consts):

        def advance(carried, pieces):
            return inner_step(carried, pieces, head_consts)
        return lax.scan(advance, start_state, (head_keys, head_values, head_queries))[1]
    return jax.vmap(one_head)(init_params, key_rows, value_rows, query_rows, consts)

def attend(query_tile, key_tile, value_tile, own_ids, near_ids):
    scores = jnp.einsum('qhd,khd->hqk', query_tile.astype(jnp.float32), key_tile.astype(jnp.float32)) * HDIM ** (-0.5)
    allowed = own_ids[:, None] == near_ids[None, :]
    scores = jnp.where(allowed[None], scores, -1e+30)
    top = lax.optimization_barrier(jnp.max(scores, -1, keepdims=True))
    expo = jnp.exp(scores - top)
    total = lax.optimization_barrier(jnp.sum(expo, -1, keepdims=True))
    weights = (expo / total).astype(jnp.bfloat16)
    return jnp.einsum('hqk,khd->qhd', weights.astype(jnp.float32), value_tile.astype(jnp.float32))

def reference(tokens, qkv_weight, out_weight, segment_ids, inner_w1, inner_b1, inner_w2, inner_b2, norm_gain, norm_bias, inner_rate, out_gate):
    projected = [jnp.dot(tokens, qkv_weight[c], preferred_element_type=jnp.float32).astype(jnp.bfloat16) for c in range(3)]
    queries = projected[0].reshape(TOKENS, HEADS, HDIM)
    keys_all = projected[1].reshape(TOKENS, HEADS, HDIM)
    values_all = projected[2].reshape(TOKENS, HEADS, HDIM)
    all_ids = segment_ids.astype(jnp.int32)
    width = min(TOKENS, 256)

    def block(index):
        start = (index * width).astype(jnp.int32)
        query_tile = lax.dynamic_slice_in_dim(queries, start, width, 0)
        own_ids = lax.dynamic_slice_in_dim(all_ids, start, width, 0)
        return attend(query_tile, keys_all, values_all, own_ids, all_ids)
    attention = lax.map(block, jnp.arange(TOKENS // width, dtype=jnp.int32)).reshape(TOKENS, HEADS, HDIM)

    def to_blocks(field):
        return jnp.transpose(field.reshape(TOKENS // GROUP, GROUP, HEADS, HDIM), (2, 0, 1, 3))

    def from_blocks(field):
        return jnp.transpose(field, (1, 2, 0, 3)).reshape(TOKENS, HEADS, HDIM)
    key_rows = rms_scaled(keys_all.astype(jnp.float32))
    value_rows = rms_scaled(values_all.astype(jnp.float32))
    query_rows = rms_scaled(queries.astype(jnp.float32))
    init_params = (inner_w1, inner_b1, inner_w2, inner_b2)
    consts = (norm_gain, norm_bias, inner_rate)
    forward = from_blocks(sweep_heads(init_params, to_blocks(key_rows), to_blocks(value_rows), to_blocks(query_rows), consts))
    backward = from_blocks(sweep_heads(init_params, to_blocks(key_rows[::-1]), to_blocks(value_rows[::-1]), to_blocks(query_rows[::-1]), consts))[::-1]
    mixed = (attention + jnp.tanh(out_gate) * (forward + backward)).astype(jnp.bfloat16).reshape(TOKENS, INNER)
    return jnp.dot(mixed, out_weight, preferred_element_type=jnp.float32).astype(jnp.bfloat16)
```

```python
import functools

import jax
import jax.numpy as jnp
from jax import lax
from jax.experimental import pallas as pl
from jax.experimental.pallas import tpu as pltpu
from jax.sharding import PartitionSpec as P

MESH = pl.DeviceIdType.MESH
F = jnp.float32
B = jnp.bfloat16
HDIM = 64
GROUP = 64
EPS = 1e-06
NN = (((1,), (0,)), ((), ()))
NT = (((1,), (1,)), ((), ()))
TN = (((0,), (0,)), ((), ()))
C0 = 0.7978845608028654
C1 = 0.044715
N_TM = 32
HEADS = 6
BLOCKS = 128
PACK = 384
KEYS = 1024
CHAINS = 2 * HEADS
PER_HEAD = 3
ROLES = CHAINS + PER_HEAD * HEADS


def mm(a, b, dims=NN):
    return lax.dot_general(a, b, dims, preferred_element_type=F)


def gelu_both(x):
    x2 = x * x
    th = jnp.tanh(x * (C0 + (C0 * C1) * x2))
    hp = 0.5 + 0.5 * th
    return x * hp, hp + (hp - hp * hp) * (x * (2 * C0 + (6 * C0 * C1) * x2))


def gelu(x):
    x2 = x * x
    th = jnp.tanh(x * (C0 + (C0 * C1) * x2))
    return x * (0.5 + 0.5 * th)


def mean(x):
    return jnp.mean(x, -1, keepdims=True)


def lanes(shape):
    return lax.broadcasted_iota(jnp.int32, shape, 1)


def chain(rev, rate, buf, w1i, w2i, b2i, gain, bias, out, W1, W2, W2b, b2):
    gn, bs = gain[...], bias[...]
    g2 = gn * gn
    s = rate / (GROUP * HDIM)
    lane = lanes((64, 128))
    tail = jnp.where(lane == 64, 1.0, 0.0).astype(B)

    def place(step):
        b = jnp.clip(step, 0, BLOCKS - 1)
        b = jnp.where(rev, BLOCKS - 1 - b, b)
        return b // 4, b % 4

    def load_ka(step):
        i, j = place(step)
        return buf[i, pl.ds(pl.multiple_of(j * 64, 64), 64), :]

    def load_q(step):
        i, j = place(step)
        both = buf[i, pl.ds(pl.multiple_of(256 + (j // 2) * 64, 64), 64), :]
        swapped = jnp.concatenate([both[:, 64:], both[:, :64]], 1)
        return jnp.where(lane < 64, jnp.where(j % 2 == 0, both, swapped), tail)

    def augment(ka):
        return jnp.where(lane < 64, ka, tail)

    W1[...] = w1i[...]
    w2 = w2i[...]
    W2[...] = w2 - jnp.mean(w2, 0, keepdims=True)
    W2b[...] = W2[...].astype(B)
    start_b2 = b2i[...]
    b2[...] = start_b2 - mean(start_b2)
    first = augment(load_ka(0))
    base0 = mm(first, W1[...].astype(B))

    def body(t, carry):
        G1, base, Pt, KTs, Kt, Zlast = carry
        A = load_ka(t)[:, 64:].astype(F)
        mA = mean(A)
        W2t = W2b[...]
        b2t = b2[...]
        AW = mm(A.astype(B), W2t)
        R = mm(jnp.concatenate([Pt, KTs], 0), G1)
        Z1 = base - R[:64]
        W1n = W1[...] - R[64:]
        W1[...] = W1n
        W1b = W1n.astype(B)
        X2, dX = gelu_both(Z1)
        X2b = X2.astype(B)
        Z = mm(X2b, W2t, NT) + b2t
        Zg = Z * g2
        D = mm(jnp.concatenate([Zg.astype(B), Z.astype(B)], 0), W2t)
        S1, S2, S3, S4 = mean(Z * Z), mean(Zg), mean(Z * Zg), mean(A * Z)
        inv = lax.rsqrt(S1 + EPS)
        a1 = inv * inv
        a3 = a1 * (a1 * S3 + inv * S4)
        G1n = ((a1 * D[:64] + inv * AW - a3 * D[64:]) * dX).astype(B)
        G2 = a1 * Zg + inv * A - a3 * Z - inv * (inv * S2 + mA)
        U = mm(G2.astype(B), X2b, TN)
        W2n = W2[...] - s * U
        W2b[...] = W2n.astype(B)
        W2[...] = W2n - jnp.mean(W2n, 0, keepdims=True)
        b2n = b2t - s * jnp.sum(G2, 0, keepdims=True)
        b2[...] = b2n - mean(b2n)
        Kn = augment(load_ka(t + 1))
        Y = mm(jnp.concatenate([load_q(t - 1), Kn], 0), W1b)
        Zq = mm(gelu(Y[:64]).astype(B), W2t, NT) + b2t
        Pn = (s * mm(Kn, Kt, NT)).astype(B)
        KTn = (s * Kt.astype(F)).T.astype(B)
        z = Zlast - mean(Zlast)
        o = (z * lax.rsqrt(mean(z * z) + EPS) * gn + bs).astype(B)
        i, j = place(t - 2)
        rows = pl.ds(pl.multiple_of((j // 2) * 64, 64), 64)
        twice = jnp.concatenate([o, o], 1)
        out[i, rows, :] = jnp.where((lane < 64) == (j % 2 == 0), twice, out[i, rows, :])
        return G1n, Y[64:], Pn, KTn, Kn, Zq

    lax.fori_loop(
        0,
        BLOCKS + 2,
        body,
        (
            jnp.zeros((64, 256), B),
            base0,
            jnp.zeros((64, 64), B),
            jnp.zeros((128, 64), B),
            first,
            jnp.zeros((64, 64), F),
        ),
    )


def attend(third, c1, c2, buf, out):
    begin = (third * N_TM + PER_HEAD - 1) // PER_HEAD
    end = ((third + 1) * N_TM + PER_HEAD - 1) // PER_HEAD
    lane = lanes((128, 128))
    low = lane < 64
    per = KEYS // 256
    ones = jnp.ones((KEYS, 128), B)

    def segment(pos):
        return jnp.where(pos >= c1, 1, 0) + jnp.where(pos >= c2, 1, 0)

    row = lax.broadcasted_iota(jnp.int32, (256, 1), 0)
    inside = (row % 128) // 64 * 128 + (row // 128) * 64 + row % 64

    def block(i, _):
        both = buf[i, 256:PACK, :]
        swapped = jnp.concatenate([both[:, 64:], both[:, :64]], 1)
        zero = jnp.zeros_like(both)
        q = jnp.concatenate([jnp.where(low, both, zero), jnp.where(low, swapped, zero)], 0)
        own = segment(i * 256 + inside)

        def keys(n, carry):
            top, acc = carry
            kv = jnp.concatenate([buf[n * per + m, 0:256, :] for m in range(per)], 0)
            scores = mm(q, kv, NT)
            ids = segment(n * KEYS + lanes((1, KEYS)))
            scores = jnp.where(own == ids, scores, -1e30)
            top_new = jnp.maximum(top, jnp.max(scores, -1, keepdims=True))
            w = jnp.exp(scores - top_new).astype(B)
            fresh = mm(w, jnp.concatenate([kv, ones], 1))
            return top_new, acc * jnp.exp(top - top_new) + fresh

        start = (jnp.full((256, 1), -1e30, F), jnp.zeros((256, 256), F))
        acc = lax.fori_loop(0, N_TM * 256 // KEYS, keys, start)[1]
        o = acc[:, :128] / acc[:, 128:]
        lo = jnp.concatenate([o[:128, 64:], o[:128, :64]], 1)
        out[i] = jnp.where(low, lo, o[128:]).astype(B)
        return 0

    lax.fori_loop(begin, end, block, 0)


def role_kernel(cut_ref, rate_ref, buf, w1, w2, b2i, gain, bias, out, W1, W2, W2b, b2):
    me = lax.axis_index("tm")

    @pl.when(me < CHAINS)
    def _():
        chain(me % 2 == 1, rate_ref[0], buf, w1, w2, b2i, gain, bias, out, W1, W2, W2b, b2)

    @pl.when((me >= CHAINS) & (me < ROLES))
    def _():
        attend((me - CHAINS) % PER_HEAD, cut_ref[0], cut_ref[1], buf, out)


def greet():
    me = lax.axis_index("tm")
    barrier = pltpu.get_barrier_semaphore()

    @pl.loop(1, N_TM)
    def _(k):
        pl.semaphore_signal(
            barrier, inc=1, device_id={"tm": lax.rem(me + k, N_TM)}, device_id_type=MESH
        )

    pl.semaphore_wait(barrier, N_TM - 1)
    return me


def spread_kernel(src, buf, send_sem, recv_sem, own_sem):
    me = greet()

    def slot(d):
        return jnp.where(d < CHAINS, d // 2, HEADS + (d - CHAINS) // PER_HEAD)

    @pl.loop(1, N_TM)
    def _(k):
        d = lax.rem(me + k, N_TM)

        @pl.when(d < ROLES)
        def _():
            pltpu.make_async_remote_copy(
                src_ref=src.at[slot(d)],
                dst_ref=buf.at[me],
                send_sem=send_sem,
                recv_sem=recv_sem,
                device_id={"tm": d},
                device_id_type=MESH,
            ).start()

    @pl.when(me < ROLES)
    def _():
        own = pltpu.make_async_copy(src.at[slot(me)], buf.at[me], own_sem)
        own.start()
        own.wait()
        rest = pl.ds(0, N_TM - 1)
        pltpu.make_async_copy(buf.at[rest], buf.at[rest], recv_sem).wait()
        sent = pl.ds(0, ROLES - 1)
        pltpu.make_async_copy(buf.at[sent], buf.at[sent], send_sem).wait()

    @pl.when(me >= ROLES)
    def _():
        sent = pl.ds(0, ROLES)
        pltpu.make_async_copy(buf.at[sent], buf.at[sent], send_sem).wait()


def gather_kernel(src, res, send_sem, recv_sem, own_sem):
    me = greet()
    total = 3 * HEADS
    is_chain = me < CHAINS
    third = (me - CHAINS) % PER_HEAD
    begin = jnp.where(is_chain, 0, (third * N_TM + PER_HEAD - 1) // PER_HEAD)
    end = jnp.where(is_chain, N_TM, ((third + 1) * N_TM + PER_HEAD - 1) // PER_HEAD)
    end = jnp.where(me < ROLES, end, begin)
    slot = jnp.where(is_chain, me, CHAINS + (me - CHAINS) // PER_HEAD)
    has_own = (me >= begin) & (me < end)

    @pl.loop(0, N_TM)
    def _(i):
        @pl.when((i >= begin) & (i < end) & (i != me))
        def _():
            pltpu.make_async_remote_copy(
                src_ref=src.at[i],
                dst_ref=res.at[slot],
                send_sem=send_sem,
                recv_sem=recv_sem,
                device_id={"tm": i},
                device_id_type=MESH,
            ).start()

    @pl.when(has_own)
    def _():
        own = pltpu.make_async_copy(src.at[me], res.at[slot], own_sem)
        own.start()
        own.wait()
        rest = pl.ds(0, total - 1)
        pltpu.make_async_copy(res.at[rest], res.at[rest], recv_sem).wait()

    @pl.when(jnp.logical_not(has_own))
    def _():
        pltpu.make_async_copy(res, res, recv_sem).wait()

    count = end - begin - jnp.where(has_own, 1, 0)
    third_size = N_TM // PER_HEAD
    for amount in (third_size - 1, third_size, third_size + 1, N_TM - 1):

        @pl.when(count == amount)
        def _():
            sent = pl.ds(0, amount)
            pltpu.make_async_copy(src.at[sent], src.at[sent], send_sem).wait()


def exchange(kernel, src, shape, name, collective_id):
    return pl.pallas_call(
        kernel,
        out_shape=jax.ShapeDtypeStruct(shape, B),
        in_specs=[pl.BlockSpec(memory_space=pl.ANY)],
        out_specs=pl.BlockSpec(memory_space=pl.ANY),
        scratch_shapes=[pltpu.SemaphoreType.DMA] * 3,
        compiler_params=pltpu.CompilerParams(collective_id=collective_id, has_side_effects=True),
        name=name,
    )(src)


def rms_scaled(field):
    return field * lax.rsqrt(jnp.mean(field * field, -1, keepdims=True) + EPS)


def pair_up(field):
    heads = field.shape[0]
    split = field.reshape(heads, 2, 2, 64, 64)
    return jnp.transpose(split, (0, 1, 3, 2, 4)).reshape(heads, 128, 128)


def unpair(packed):
    count = packed.shape[0]
    split = packed.reshape(count, 2, 64, 2, 64)
    return jnp.transpose(split, (0, 1, 3, 2, 4)).reshape(count, 256, 64)


def run_roles(buf, cut, rate, w1, w2, b2, gain, bias):
    sm = pl.BlockSpec(memory_space=pltpu.SMEM)
    vm = pl.BlockSpec(memory_space=pltpu.VMEM)
    return pl.pallas_call(
        role_kernel,
        out_shape=jax.ShapeDtypeStruct((N_TM, 128, 128), B),
        in_specs=[sm, sm] + [vm] * 6,
        out_specs=vm,
        scratch_shapes=[
            pltpu.VMEM((128, 256), F),
            pltpu.VMEM((64, 256), F),
            pltpu.VMEM((64, 256), B),
            pltpu.VMEM((1, 64), F),
        ],
        compiler_params=pltpu.CompilerParams(vmem_limit_bytes=48 * 2**20),
        name="roles",
    )(cut, rate, buf, w1, w2, b2, gain, bias)


def local(
    tokens,
    qkv_weight,
    out_weight,
    segment_ids,
    inner_w1,
    inner_b1,
    inner_w2,
    inner_b2,
    norm_gain,
    norm_bias,
    inner_rate,
    out_gate,
):
    rows = tokens.shape[0]
    heads = inner_w1.shape[0]
    me = lax.axis_index("tm")
    projected = jnp.einsum(
        "tw,cwf->ctf",
        lax.all_gather(tokens, "head", axis=1, tiled=True),
        qkv_weight,
        preferred_element_type=F,
    ).astype(B)
    by_head = jnp.transpose(projected.reshape(3, rows, heads, HDIM), (0, 2, 1, 3))
    query, key, value = by_head[0], by_head[1], by_head[2]
    query_rows = rms_scaled(query.astype(F))
    key_rows = rms_scaled(key.astype(F))
    value_rows = rms_scaled(value.astype(F))
    aim = (norm_bias[:, None] - (value_rows - key_rows)) * norm_gain[:, None]
    for_chain = jnp.concatenate(
        [
            jnp.concatenate([key_rows.astype(B), aim.astype(B)], 2),
            pair_up(query_rows.astype(B)),
        ],
        1,
    )
    for_attention = jnp.concatenate(
        [jnp.concatenate([key, value], 2), pair_up(query * jnp.asarray(HDIM**-0.5, B))], 1
    )
    buf = exchange(
        spread_kernel,
        jnp.concatenate([for_chain, for_attention], 0),
        (N_TM, PACK, 128),
        "spread",
        1,
    )
    head = jnp.where(me < CHAINS, me // 2, 0)

    def pick(array):
        return lax.dynamic_index_in_dim(array, head, 0, keepdims=False)

    w1 = jnp.concatenate([pick(inner_w1), pick(inner_b1)[None], jnp.zeros((63, 256), F)], 0)
    cut = jnp.stack([jnp.sum(segment_ids < 1), jnp.sum(segment_ids < 2)]).astype(jnp.int32)
    done = run_roles(
        buf,
        cut,
        pick(inner_rate).reshape(1),
        w1,
        pick(inner_w2).T,
        pick(inner_b2)[None],
        pick(norm_gain)[None],
        pick(norm_bias)[None],
    )
    res = unpair(exchange(gather_kernel, done, (3 * HEADS, 128, 128), "collect", 2)).astype(F)
    sweeps = res[:CHAINS].reshape(heads, 2, rows, HDIM)
    swept = sweeps[:, 0] + sweeps[:, 1] + 2.0 * query_rows
    mixed = (res[CHAINS:] + jnp.tanh(out_gate)[:, None] * swept).astype(B)
    mixed = jnp.transpose(mixed, (1, 0, 2)).reshape(rows, heads * HDIM)
    terms = jnp.dot(mixed, out_weight, preferred_element_type=F)
    return lax.psum_scatter(terms.astype(B), "head", scatter_dimension=1, tiled=True)


def solution(mesh):
    placed = (
        P("tm", "head"),
        P(None, None, "head"),
        P("head", None),
        P(),
        P("head", None, None),
        P("head", None),
        P("head", None, None),
        P("head", None),
        P("head", None),
        P("head", None),
        P("head"),
        P("head", None),
    )
    return jax.shard_map(
        local, mesh=mesh, in_specs=placed, out_specs=P("tm", "head"), check_vma=False
    )
```

```python
import jax
import jax.numpy as jnp
from jax import lax
from jax.experimental import pallas as pl
from jax.experimental.pallas import tpu as pltpu
from jax.sharding import PartitionSpec as P

MESH = pl.DeviceIdType.MESH
F = jnp.float32
B = jnp.bfloat16
HDIM = 64
GROUP = 64
EPS = 1e-06
NN = (((1,), (0,)), ((), ()))
NT = (((1,), (1,)), ((), ()))
TN = (((0,), (0,)), ((), ()))
C0 = 0.7978845608028654
C1 = 0.044715
N_TM = 32
HEADS = 6
BLOCKS = 128
PACK = 384
KEYS = 2048
CHAINS = 2 * HEADS
PER_HEAD = 3
ROLES = CHAINS + PER_HEAD * HEADS
N_HEAD = 8
WIDTH = HEADS * HDIM


def mm(a, b, dims=NN):
    return lax.dot_general(a, b, dims, preferred_element_type=F)


def gelu_both(x):
    x2 = x * x
    th = jnp.tanh(x * (C0 + (C0 * C1) * x2))
    hp = 0.5 + 0.5 * th
    return x * hp, hp + (hp - hp * hp) * (x * (2 * C0 + (6 * C0 * C1) * x2))


def gelu(x):
    x2 = x * x
    th = jnp.tanh(x * (C0 + (C0 * C1) * x2))
    return x * (0.5 + 0.5 * th)


def mean(x):
    return jnp.mean(x, -1, keepdims=True)


def lanes(shape):
    return lax.broadcasted_iota(jnp.int32, shape, 1)


def chain(rev, rate, buf, w1, b1, w2, b2i, gn, bs, out, W1, W2, W2b, b2, arrived, finished):
    g2 = gn * gn
    s = rate / (GROUP * HDIM)
    lane = lanes((64, 128))
    tail = jnp.where(lane == 64, 1.0, 0.0).astype(B)

    def place(step):
        b = jnp.clip(step, 0, BLOCKS - 1)
        b = jnp.where(rev, BLOCKS - 1 - b, b)
        return b // 4, b % 4

    def load_ka(step):
        i, j = place(step)
        return buf[i, pl.ds(pl.multiple_of(j * 64, 64), 64), :]

    def load_q(step):
        i, j = place(step)
        both = buf[i, pl.ds(pl.multiple_of(256 + (j // 2) * 64, 64), 64), :]
        swapped = jnp.concatenate([both[:, 64:], both[:, :64]], 1)
        return jnp.where(lane < 64, jnp.where(j % 2 == 0, both, swapped), tail)

    def augment(ka):
        return jnp.where(lane < 64, ka, tail)

    arrived(0)
    W1[0:64] = w1
    W1[64:128] = jnp.where(lax.broadcasted_iota(jnp.int32, (64, 256), 0) == 0, b1, 0.0)
    w2 = w2.T
    W2[...] = w2 - jnp.mean(w2, 0, keepdims=True)
    W2b[...] = W2[...].astype(B)
    valid = lane < 64
    valid_row = lanes((1, 128)) < 64

    def widen(x):
        return jnp.concatenate([x, jnp.zeros_like(x)], 1)

    def swap(x):
        return jnp.concatenate([x[:, 64:], x[:, :64]], 1)

    def rowsum(x):
        return jnp.sum(x, -1, keepdims=True) * (1.0 / HDIM)

    b2[...] = widen(b2i - mean(b2i))
    gn, bs, g2 = widen(gn), widen(bs), widen(g2)
    first = augment(load_ka(0))
    base0 = mm(first, W1[...].astype(B))
    zero_rows = jnp.zeros((64, 256), B)

    def body(t, carry):
        G1, base, Pt, KTs, Kt, Zlast = carry
        Ab = jnp.where(valid, swap(load_ka(t)), jnp.zeros((64, 128), B))
        A = Ab.astype(F)
        W2t = W2b[...]
        W2z = jnp.concatenate([W2t, zero_rows], 0)
        b2t = b2[...]
        AW = mm(Ab[:, :64], W2t)
        R = mm(jnp.concatenate([Pt, KTs], 0), G1)
        Z1 = base - R[:64]
        W1n = W1[...] - R[64:]
        W1[...] = W1n
        W1b = W1n.astype(B)
        X2, dX = gelu_both(Z1)
        X2b = X2.astype(B)
        Z = mm(X2b, W2z, NT) + b2t
        Zg = Z * g2
        D = mm(jnp.concatenate([Zg.astype(B), Z.astype(B)], 0)[:, :64], W2t)
        mA = rowsum(A)
        S1, S2, S3, S4 = rowsum(Z * Z), rowsum(Zg), rowsum(Z * Zg), rowsum(A * Z)
        inv = lax.rsqrt(S1 + EPS)
        a1 = inv * inv
        a3 = a1 * (a1 * S3 + inv * S4)
        G1n = ((a1 * D[:64] + inv * AW - a3 * D[64:]) * dX).astype(B)
        G2 = a1 * Zg + inv * A - a3 * Z - inv * (inv * S2 + mA)
        U = mm(G2.astype(B)[:, :64], X2b, TN)
        W2n = W2[...] - s * U
        W2b[...] = W2n.astype(B)
        W2[...] = W2n - jnp.mean(W2n, 0, keepdims=True)
        b2n = jnp.where(valid_row, b2t - s * jnp.sum(G2, 0, keepdims=True), 0.0)
        b2[...] = jnp.where(valid_row, b2n - rowsum(b2n), 0.0)
        Kn = augment(load_ka(t + 1))
        Y = mm(jnp.concatenate([load_q(t - 1), Kn], 0), W1b)
        Zq = mm(gelu(Y[:64]).astype(B), W2z, NT) + b2t
        Pn = (s * mm(Kn, Kt, NT)).astype(B)
        KTn = (s * Kt.astype(F)).T.astype(B)
        z = jnp.where(valid, Zlast - rowsum(Zlast), 0.0)
        o = (z * lax.rsqrt(rowsum(z * z) + EPS) * gn + bs).astype(B)
        i, j = place(t - 2)
        rows = pl.ds(pl.multiple_of((j // 2) * 64, 64), 64)
        out[i, rows, :] = jnp.where(valid == (j % 2 == 0), jnp.where(j % 2 == 0, o, swap(o)), out[i, rows, :])
        return G1n, Y[64:], Pn, KTn, Kn, Zq

    def group(i, carry):
        @pl.when(i + 1 < N_TM)
        def _():
            arrived(i + 1)

        carry = lax.fori_loop(4 * i, 4 * i + 4, body, carry)

        @pl.when(i > 0)
        def _():
            finished(i - 1)

        return carry

    carry = lax.fori_loop(
        0,
        N_TM,
        group,
        (
            jnp.zeros((64, 256), B),
            base0,
            jnp.zeros((64, 64), B),
            jnp.zeros((128, 64), B),
            first,
            jnp.zeros((64, 128), F),
        ),
    )
    lax.fori_loop(BLOCKS, BLOCKS + 2, body, carry)
    finished(N_TM - 1)


def third_begin(third):
    return (third * N_TM + PER_HEAD - 1) // PER_HEAD


def attend(third, ids, buf, out, finished):
    begin, end = third_begin(third), third_begin(third + 1)
    lane = lanes((128, 128))
    low = lane < 64
    per = KEYS // 256

    def count(flags):
        ones_of = jnp.where(flags, 1.0, 0.0)
        return jnp.sum(jnp.sum(ones_of, 0, keepdims=True), 1, keepdims=True)

    c1, c2 = count(ids < 1), count(ids < 2)

    def segment(pos):
        pos = pos.astype(F)
        return jnp.where(pos >= c1, 1.0, 0.0) + jnp.where(pos >= c2, 1.0, 0.0)

    row = lax.broadcasted_iota(jnp.int32, (256, 1), 0)
    inside = (row % 128) // 64 * 128 + (row // 128) * 64 + row % 64

    def block(i, _):
        both = buf[i, 256:PACK, :]
        swapped = jnp.concatenate([both[:, 64:], both[:, :64]], 1)
        zero = jnp.zeros_like(both)
        q = jnp.concatenate([jnp.where(low, both, zero), jnp.where(low, swapped, zero)], 0)
        own = segment(i * 256 + inside)

        def keys(n, carry):
            top, acc, total = carry
            kv = jnp.concatenate([buf[n * per + m, 0:256, :] for m in range(per)], 0)
            scores = mm(q, kv, NT)
            ids = segment(n * KEYS + lanes((1, KEYS)))
            scores = jnp.where(own == ids, scores, -1e30)
            top_new = jnp.maximum(top, jnp.max(scores, -1, keepdims=True))
            w = jnp.exp(scores - top_new)
            fade = jnp.exp(top - top_new)
            total = total * fade + jnp.sum(w, -1, keepdims=True)
            return top_new, acc * fade + mm(w.astype(B), kv), total

        start = (jnp.full((256, 1), -1e30, F), jnp.zeros((256, 128), F), jnp.zeros((256, 1), F))
        _, acc, total = lax.fori_loop(0, N_TM * 256 // KEYS, keys, start)
        o = acc / total
        lo = jnp.concatenate([o[:128, 64:], o[:128, :64]], 1)
        out[i] = jnp.where(low, lo, o[128:]).astype(B)
        finished(i)
        return 0

    lax.fori_loop(begin, end, block, 0)


def greet(axis):
    me, n = lax.axis_index(axis), lax.axis_size(axis)
    barrier = pltpu.get_barrier_semaphore()

    @pl.loop(1, n)
    def _(k):
        pl.semaphore_signal(
            barrier, inc=1, device_id={axis: lax.rem(me + k, n)}, device_id_type=MESH
        )

    pl.semaphore_wait(barrier, n - 1)
    return me


def slot_of(d):
    return jnp.where(d < CHAINS, d // 2, HEADS + (d - CHAINS) // PER_HEAD)


def with_queries(block, d):
    third = (d - CHAINS) % PER_HEAD
    return (d < CHAINS) | ((block >= third_begin(third)) & (block < third_begin(third + 1)))


def sweep_kernel(
    src, rate, ids, w1, b1, w2, b2i, gain, bias, res,
    buf, out, W1, W2, W2b, b2, send_sem, recv_sem, own_sem, res_send, res_recv,
):
    me = greet("tm")
    short = pl.ds(0, 256)

    def parcel(d, part):
        slot = slot_of(d)
        return pltpu.make_async_remote_copy(
            src_ref=src.at[slot, short] if part else src.at[slot],
            dst_ref=buf.at[me, short] if part else buf.at[me],
            send_sem=send_sem.at[d],
            recv_sem=recv_sem.at[me],
            device_id={"tm": d},
            device_id_type=MESH,
        )

    def each(first, count, stride, act):
        @pl.loop(0, count)
        def _(k):
            d = first + stride * k

            @pl.when(d != me)
            def _():
                act(d)

    def start(d):
        @pl.when(with_queries(me, d))
        def _():
            parcel(d, False).start()

        @pl.when(jnp.logical_not(with_queries(me, d)))
        def _():
            parcel(d, True).start()

    def sent(d):
        @pl.when(with_queries(me, d))
        def _():
            parcel(d, False).wait_send()

        @pl.when(jnp.logical_not(with_queries(me, d)))
        def _():
            parcel(d, True).wait_send()

    @pl.when(me < ROLES)
    def _():
        own = pltpu.make_async_copy(src.at[slot_of(me)], buf.at[me], own_sem)
        own.start()
        own.wait()

    early, late = me < 8, me >= 24
    each(jnp.where(late, 1, 0), jnp.where(early | late, HEADS, 0), 2, start)
    each(CHAINS, PER_HEAD * HEADS, 1, start)
    each(jnp.where(me < 16, 0, 1), jnp.where(early | late, 0, HEADS), 2, start)
    each(jnp.where(me < 16, 1, 0), HEADS, 2, start)

    def landed(i):
        @pl.when(i != me)
        def _():
            @pl.when(with_queries(i, me))
            def _():
                pltpu.make_async_copy(buf.at[i], buf.at[i], recv_sem.at[i]).wait()

            @pl.when(jnp.logical_not(with_queries(i, me)))
            def _():
                got = buf.at[i, short]
                pltpu.make_async_copy(got, got, recv_sem.at[i]).wait()

    slot = jnp.where(me < CHAINS, me, CHAINS + (me - CHAINS) // PER_HEAD)

    def away(i):
        return pltpu.make_async_remote_copy(
            src_ref=out.at[i],
            dst_ref=res.at[slot],
            send_sem=res_send.at[i],
            recv_sem=res_recv.at[slot],
            device_id={"tm": i},
            device_id_type=MESH,
        )

    def here(i):
        return pltpu.make_async_copy(out.at[i], res.at[slot], res_send.at[i])

    def deliver(i):
        @pl.when(i != me)
        def _():
            away(i).start()

        @pl.when(i == me)
        def _():
            here(i).start()

    def delivered(i):
        @pl.when(i != me)
        def _():
            away(i).wait_send()

        @pl.when(i == me)
        def _():
            here(i).wait()

    @pl.when(me < CHAINS)
    def _():
        rev = me % 2 == 1
        head = me // 2
        row = pl.ds(head, 1)

        def real(i):
            return jnp.where(rev, N_TM - 1 - i, i)

        chain(
            rev, rate[head], buf, w1[head], b1[row, :], w2[head], b2i[row, :], gain[row, :], bias[row, :],
            out, W1, W2, W2b, b2, lambda i: landed(real(i)), lambda i: deliver(real(i)),
        )
        pl.loop(0, N_TM)(delivered)

    @pl.when((me >= CHAINS) & (me < ROLES))
    def _():
        third = (me - CHAINS) % PER_HEAD
        pl.loop(0, N_TM)(landed)
        attend(third, ids[...], buf, out, deliver)
        pl.loop(third_begin(third), third_begin(third + 1))(delivered)

    each(0, ROLES, 1, sent)

    @pl.loop(0, 3 * HEADS)
    def _(slot):
        third = jnp.where(me < third_begin(1), 0, jnp.where(me < third_begin(2), 1, 2))
        origin = jnp.where(slot < CHAINS, slot, CHAINS + (slot - CHAINS) * PER_HEAD + third)

        @pl.when(origin != me)
        def _():
            pltpu.make_async_copy(res.at[slot], res.at[slot], res_recv.at[slot]).wait()


def tile_row(ref, g):
    return jnp.concatenate([ref[2 * g : 2 * g + 1, :], ref[2 * g + 1 : 2 * g + 2, :]], 1)


def swap_halves(x):
    return jnp.concatenate([x[:, 64:], x[:, :64]], 1)


def project_kernel(tok, w_hbm, gain, bias, src, qrows, toks, w, acc, send_sem, recv_sem, w_sem):
    me = lax.axis_index("head")
    fetch = pltpu.make_async_copy(w_hbm, w, w_sem)
    fetch.start()
    greet("head")

    def parcel(k):
        return pltpu.make_async_remote_copy(
            src_ref=tok,
            dst_ref=toks.at[me],
            send_sem=send_sem.at[k],
            recv_sem=recv_sem.at[me],
            device_id={"head": lax.rem(me + k, N_HEAD)},
            device_id_type=MESH,
        )

    pl.loop(1, N_HEAD)(lambda k: parcel(k).start())
    fetch.wait()

    def add(x, s, fresh):
        rows = pl.ds(pl.multiple_of(s * WIDTH, WIDTH), WIDTH)
        for c in range(3):
            cols = slice(c * WIDTH, (c + 1) * WIDTH)
            y = mm(x, w[c, rows, :])
            acc[:, cols] = y if fresh else acc[:, cols] + y

    add(tok[...], me, True)

    @pl.loop(1, N_HEAD)
    def _(k):
        s = lax.rem(me + N_HEAD - k, N_HEAD)
        pltpu.make_async_copy(toks.at[s], toks.at[s], recv_sem.at[s]).wait()
        add(toks[s], s, False)

    low = lanes((256, 128)) < 64
    low_half = lanes((128, 128)) < 64
    r = lax.broadcasted_iota(jnp.int32, (128, 128), 0)
    same = jnp.where((r < 64) == low_half, 1.0 / HDIM, 0.0).astype(B)

    def scaled(x):
        sq = x * x
        hi = sq.astype(B)
        return x * lax.rsqrt(mm(hi, same) + mm((sq - hi.astype(F)).astype(B), same) + EPS)

    def pack_rows(left, right):
        pairs = [jnp.where(low, left, swap_halves(right)), jnp.where(low, swap_halves(left), right)]
        return pairs

    def pack_pairs(x):
        y = swap_halves(x)
        even = [jnp.where(low[:64], x[a : a + 64], y[a + 64 : a + 128]) for a in (0, 128)]
        odd = [jnp.where(low[:64], y[a : a + 64], x[a + 64 : a + 128]) for a in (0, 128)]
        return jnp.concatenate(even, 0), jnp.concatenate(odd, 0)

    for g in range(HEADS // 2):
        q, k, v = (
            acc[:, c * WIDTH + g * 128 : c * WIDTH + (g + 1) * 128].astype(B).astype(F) for c in range(3)
        )
        qn, kn, vn = scaled(q), scaled(k), scaled(v)
        qrows[:, g * 128 : (g + 1) * 128] = qn
        aim = (tile_row(bias, g) - (vn - kn)) * tile_row(gain, g)
        sets = ((kn, aim, qn, 0), (k, v, q * HDIM**-0.5, HEADS))
        for left, right, quer, offset in sets:
            tops, tails = pack_rows(left, right), pack_pairs(quer)
            for e in range(2):
                src[offset + 2 * g + e, 0:256, :] = tops[e].astype(B)
                src[offset + 2 * g + e, 256:PACK, :] = tails[e].astype(B)

    pl.loop(1, N_HEAD)(lambda k: parcel(k).wait_send())


def finish_kernel(res, qrows, gate, w, out, mixed, terms, got, send_sem, recv_sem):
    me = greet("head")
    low = lanes((64, 128)) < 64
    for g in range(HEADS // 2):
        weight = jnp.tanh(tile_row(gate, g))
        for p in range(2):
            rows = slice(p * 64, p * 64 + 64)
            both = []
            for e in range(2):
                h = 2 * g + e
                swept = res[2 * h, rows, :].astype(F) + res[2 * h + 1, rows, :].astype(F)
                both.append((swept, res[CHAINS + h, rows, :].astype(F)))
            for c in range(2):
                at = slice((2 * p + c) * 64, (2 * p + c + 1) * 64)
                swept, attention = (
                    jnp.where(low, x, swap_halves(y)) if c == 0 else jnp.where(low, swap_halves(x), y)
                    for x, y in zip(both[0], both[1])
                )
                cols = slice(g * 128, g * 128 + 128)
                mixed[at, cols] = (attention + weight * (swept + 2.0 * qrows[at, cols])).astype(B)

    def part(d):
        cols = pl.ds(pl.multiple_of(d * WIDTH, WIDTH), WIDTH)
        return mm(mixed[...], w[:, cols])

    def parcel(k):
        return pltpu.make_async_remote_copy(
            src_ref=terms.at[k],
            dst_ref=got.at[me],
            send_sem=send_sem.at[k],
            recv_sem=recv_sem.at[me],
            device_id={"head": lax.rem(me + k, N_HEAD)},
            device_id_type=MESH,
        )

    @pl.loop(1, N_HEAD)
    def _(k):
        terms[k] = part(lax.rem(me + k, N_HEAD)).astype(B)
        parcel(k).start()

    def gather(k, total):
        s = lax.rem(me + N_HEAD - k, N_HEAD)
        pltpu.make_async_copy(got.at[s], got.at[s], recv_sem.at[s]).wait()
        return total + got[s].astype(F)

    out[...] = lax.fori_loop(1, N_HEAD, gather, part(me)).astype(B)
    pl.loop(1, N_HEAD)(lambda k: parcel(k).wait_send())


def call(kernel, shapes, memory, scratch, name, collective_id):
    several = len(shapes) > 1
    spaces = {"v": pltpu.VMEM, "s": pltpu.SMEM, "h": pl.ANY}
    ins, outs = memory
    specs = [pl.BlockSpec(memory_space=spaces[m]) for m in outs]
    return pl.pallas_call(
        kernel,
        out_shape=shapes if several else shapes[0],
        in_specs=[pl.BlockSpec(memory_space=spaces[m]) for m in ins],
        out_specs=specs if several else specs[0],
        scratch_shapes=scratch,
        compiler_params=pltpu.CompilerParams(
            collective_id=collective_id, has_side_effects=True, vmem_limit_bytes=48 * 2**20
        ),
        name=name,
    )


def local(
    tokens,
    qkv_weight,
    out_weight,
    segment_ids,
    inner_w1,
    inner_b1,
    inner_w2,
    inner_b2,
    norm_gain,
    norm_bias,
    inner_rate,
    out_gate,
):
    rows = tokens.shape[0]
    dma = pltpu.SemaphoreType.DMA
    src, qrows = call(
        project_kernel,
        [
            jax.ShapeDtypeStruct((2 * HEADS, PACK, 128), B),
            jax.ShapeDtypeStruct((rows, WIDTH), F),
        ],
        ("vhvv", "vv"),
        [
            pltpu.VMEM((N_HEAD, rows, WIDTH), B),
            pltpu.VMEM(qkv_weight.shape, B),
            pltpu.VMEM((rows, 3 * WIDTH), F),
            dma((N_HEAD,)),
            dma((N_HEAD,)),
            dma,
        ],
        "project",
        1,
    )(tokens, qkv_weight, norm_gain, norm_bias)
    res = call(
        sweep_kernel,
        [jax.ShapeDtypeStruct((3 * HEADS, 128, 128), B)],
        ("vs" + "v" * 7, "h"),
        [
            pltpu.VMEM((N_TM, PACK, 128), B),
            pltpu.VMEM((N_TM, 128, 128), B),
            pltpu.VMEM((128, 256), F),
            pltpu.VMEM((64, 256), F),
            pltpu.VMEM((64, 256), B),
            pltpu.VMEM((1, 128), F),
            dma((N_TM,)),
            dma((N_TM,)),
            dma,
            dma((N_TM,)),
            dma((3 * HEADS,)),
        ],
        "sweep",
        2,
    )(
        src,
        inner_rate,
        segment_ids.reshape(64, 128),
        inner_w1,
        inner_b1,
        inner_w2,
        inner_b2,
        norm_gain,
        norm_bias,
    )
    return call(
        finish_kernel,
        [jax.ShapeDtypeStruct((rows, WIDTH), B)],
        ("vvvv", "v"),
        [
            pltpu.VMEM((rows, WIDTH), B),
            pltpu.VMEM((N_HEAD, rows, WIDTH), B),
            pltpu.VMEM((N_HEAD, rows, WIDTH), B),
            dma((N_HEAD,)),
            dma((N_HEAD,)),
        ],
        "finish",
        3,
    )(res, qrows, out_gate, out_weight)


def solution(mesh):
    placed = (
        P("tm", "head"),
        P(None, None, "head"),
        P("head", None),
        P(),
        P("head", None, None),
        P("head", None),
        P("head", None, None),
        P("head", None),
        P("head", None),
        P("head", None),
        P("head"),
        P("head", None),
    )
    return jax.shard_map(
        local, mesh=mesh, in_specs=placed, out_specs=P("tm", "head"), check_vma=False
    )
```

```python
import jax
import jax.numpy as jnp
from jax import lax
from jax.experimental import pallas as pl
from jax.experimental.pallas import tpu as pltpu
from jax.sharding import PartitionSpec as P

MESH = pl.DeviceIdType.MESH
F = jnp.float32
B = jnp.bfloat16
HDIM = 64
GROUP = 64
EPS = 1e-06
NN = (((1,), (0,)), ((), ()))
NT = (((1,), (1,)), ((), ()))
TN = (((0,), (0,)), ((), ()))
C0 = 0.7978845608028654
C1 = 0.044715
N_TM = 32
HEADS = 6
BLOCKS = 128
PACK = 384
CHAINS = 2 * HEADS
PLACES = 2 * HEADS
HALF = N_TM // 2
WINDOW = 4096 // 256 + 1
UNITS = HALF + 2
FAR = 1 << 20
N_HEAD = 8
WIDTH = HEADS * HDIM


def mm(a, b, dims=NN):
    return lax.dot_general(a, b, dims, preferred_element_type=F)


def gelu_both(x):
    x2 = x * x
    th = jnp.tanh(x * (C0 + (C0 * C1) * x2))
    hp = 0.5 + 0.5 * th
    return x * hp, hp + (hp - hp * hp) * (x * (2 * C0 + (6 * C0 * C1) * x2))


def gelu(x):
    x2 = x * x
    th = jnp.tanh(x * (C0 + (C0 * C1) * x2))
    return x * (0.5 + 0.5 * th)


def mean(x):
    return jnp.mean(x, -1, keepdims=True)


def lanes(shape):
    return lax.broadcasted_iota(jnp.int32, shape, 1)


def chain(rev, rate, buf, w1, b1, w2, b2i, gn, bs, out, W1, W2, W2b, b2, arrived, finished):
    g2 = gn * gn
    s = rate / (GROUP * HDIM)
    lane = lanes((64, 128))
    tail = jnp.where(lane == 64, 1.0, 0.0).astype(B)

    def place(step):
        b = jnp.clip(step, 0, BLOCKS - 1)
        b = jnp.where(rev, BLOCKS - 1 - b, b)
        return b // 4, b % 4

    def load_ka(step):
        i, j = place(step)
        return buf[i, pl.ds(pl.multiple_of(j * 64, 64), 64), :]

    def load_q(step):
        i, j = place(step)
        both = buf[i, pl.ds(pl.multiple_of(256 + (j // 2) * 64, 64), 64), :]
        swapped = jnp.concatenate([both[:, 64:], both[:, :64]], 1)
        return jnp.where(lane < 64, jnp.where(j % 2 == 0, both, swapped), tail)

    def augment(ka):
        return jnp.where(lane < 64, ka, tail)

    arrived(0)
    W1[0:64] = w1
    W1[64:128] = jnp.where(lax.broadcasted_iota(jnp.int32, (64, 256), 0) == 0, b1, 0.0)
    w2 = w2.T
    W2[...] = w2 - jnp.mean(w2, 0, keepdims=True)
    W2b[...] = W2[...].astype(B)
    valid = lane < 64
    valid_row = lanes((1, 128)) < 64

    def widen(x):
        return jnp.concatenate([x, jnp.zeros_like(x)], 1)

    def swap(x):
        return jnp.concatenate([x[:, 64:], x[:, :64]], 1)

    def rowsum(x):
        return jnp.sum(x, -1, keepdims=True) * (1.0 / HDIM)

    b2[...] = widen(b2i - mean(b2i))
    gn, bs, g2 = widen(gn), widen(bs), widen(g2)
    first = augment(load_ka(0))
    base0 = mm(first, W1[...].astype(B))
    zero_rows = jnp.zeros((64, 256), B)

    def body(t, carry):
        G1, base, Pt, KTs, Kt, Zlast = carry
        Ab = jnp.where(valid, swap(load_ka(t)), jnp.zeros((64, 128), B))
        A = Ab.astype(F)
        W2t = W2b[...]
        W2z = jnp.concatenate([W2t, zero_rows], 0)
        b2t = b2[...]
        AW = mm(Ab[:, :64], W2t)
        R = mm(jnp.concatenate([Pt, KTs], 0), G1)
        Z1 = base - R[:64]
        W1n = W1[...] - R[64:]
        W1[...] = W1n
        W1b = W1n.astype(B)
        X2, dX = gelu_both(Z1)
        X2b = X2.astype(B)
        Z = mm(X2b, W2z, NT) + b2t
        Zg = Z * g2
        D = mm(jnp.concatenate([Zg.astype(B), Z.astype(B)], 0)[:, :64], W2t)
        mA = rowsum(A)
        S1, S2, S3, S4 = rowsum(Z * Z), rowsum(Zg), rowsum(Z * Zg), rowsum(A * Z)
        inv = lax.rsqrt(S1 + EPS)
        a1 = inv * inv
        a3 = a1 * (a1 * S3 + inv * S4)
        G1n = ((a1 * D[:64] + inv * AW - a3 * D[64:]) * dX).astype(B)
        G2 = a1 * Zg + inv * A - a3 * Z - inv * (inv * S2 + mA)
        U = mm(G2.astype(B)[:, :64], X2b, TN)
        W2n = W2[...] - s * U
        W2b[...] = W2n.astype(B)
        W2[...] = W2n - jnp.mean(W2n, 0, keepdims=True)
        b2n = jnp.where(valid_row, b2t - s * jnp.sum(G2, 0, keepdims=True), 0.0)
        b2[...] = jnp.where(valid_row, b2n - rowsum(b2n), 0.0)
        Kn = augment(load_ka(t + 1))
        Y = mm(jnp.concatenate([load_q(t - 1), Kn], 0), W1b)
        Zq = mm(gelu(Y[:64]).astype(B), W2z, NT) + b2t
        Pn = (s * mm(Kn, Kt, NT)).astype(B)
        KTn = (s * Kt.astype(F)).T.astype(B)
        z = jnp.where(valid, Zlast - rowsum(Zlast), 0.0)
        o = (z * lax.rsqrt(rowsum(z * z) + EPS) * gn + bs).astype(B)
        i, j = place(t - 2)
        rows = pl.ds(pl.multiple_of((j // 2) * 64, 64), 64)
        out[i, rows, :] = jnp.where(valid == (j % 2 == 0), jnp.where(j % 2 == 0, o, swap(o)), out[i, rows, :])
        return G1n, Y[64:], Pn, KTn, Kn, Zq

    def group(i, carry):
        @pl.when(i + 1 < N_TM)
        def _():
            arrived(i + 1)

        carry = lax.fori_loop(4 * i, 4 * i + 4, body, carry)

        @pl.when(i > 0)
        def _():
            finished(i - 1)

        return carry

    carry = lax.fori_loop(
        0,
        N_TM,
        group,
        (
            jnp.zeros((64, 256), B),
            base0,
            jnp.zeros((64, 64), B),
            jnp.zeros((128, 64), B),
            first,
            jnp.zeros((64, 128), F),
        ),
    )
    lax.fori_loop(BLOCKS, BLOCKS + 2, body, carry)
    finished(N_TM - 1)


def first_at_least(ids, value):
    found = jnp.int32(0)
    for bit in range(13, -1, -1):
        trial = found + (1 << bit)
        last = ids[jnp.minimum(trial, N_TM * 256) - 1]
        found = jnp.where((trial <= N_TM * 256) & (last < value), trial, found)
    return found


def attend(half, ids, buf, parts, out, finished):
    c1, c2 = first_at_least(ids, 1), first_at_least(ids, 2)
    begin = half * HALF
    low = lanes((128, 128)) < 64
    row = lax.broadcasted_iota(jnp.int32, (256, 1), 0)
    inside = (row % 128) // 64 * 128 + (row // 128) * 64 + row % 64

    def segment(pos):
        return jnp.where(pos >= c1, 1, 0) + jnp.where(pos >= c2, 1, 0)

    def edge(number):
        return jnp.where(number <= 0, 0, jnp.where(number == 1, c1, jnp.where(number == 2, c2, FAR)))

    s0 = segment(begin * 256)
    next1, next2 = edge(s0 + 1) // 256, edge(s0 + 2) // 256

    def unit(u, _):
        above = jnp.where(begin + u - 1 >= next1, 1, 0) + jnp.where(begin + u - 2 >= next2, 1, 0)
        i = jnp.clip(begin + u - above, begin, begin + HALF - 1)
        left, right = edge(s0 + above), edge(s0 + above + 1)
        first = jnp.minimum(left // 256, N_TM - WINDOW)
        both = buf[i, 256:PACK, :]
        swapped = jnp.concatenate([both[:, 64:], both[:, :64]], 1)
        zero = jnp.zeros_like(both)
        q = jnp.concatenate([jnp.where(low, both, zero), jnp.where(low, swapped, zero)], 0)
        kv = buf[pl.ds(first, WINDOW), 0:256, :].reshape(WINDOW * 256, 128)
        pos = first * 256 + lanes((1, WINDOW * 256))
        scores = mm(q, kv, NT) + jnp.where((pos >= left) & (pos < right), 0.0, -1e30)
        w = jnp.exp(scores - jnp.max(scores, -1, keepdims=True))
        total = jnp.sum(w, -1, keepdims=True)
        parts[u] = mm(w.astype(B), kv) / total
        return 0

    lax.fori_loop(0, UNITS, unit, 0)

    def assemble(i, _):
        s1 = segment(i * 256)
        mine = segment(i * 256 + inside) - s1
        u = i - begin + s1 - s0
        o = jnp.where(
            mine == 0,
            parts[jnp.minimum(u, UNITS - 1)],
            jnp.where(
                mine == 1, parts[jnp.minimum(u + 1, UNITS - 1)], parts[jnp.minimum(u + 2, UNITS - 1)]
            ),
        )
        lo = jnp.concatenate([o[:128, 64:], o[:128, :64]], 1)
        out[i] = jnp.where(low, lo, o[128:]).astype(B)
        finished(i)
        return 0

    lax.fori_loop(begin, begin + HALF, assemble, 0)


def greet(axis):
    me, n = lax.axis_index(axis), lax.axis_size(axis)
    barrier = pltpu.get_barrier_semaphore()

    @pl.loop(1, n)
    def _(k):
        pl.semaphore_signal(
            barrier, inc=1, device_id={axis: lax.rem(me + k, n)}, device_id_type=MESH
        )

    pl.semaphore_wait(barrier, n - 1)
    return me


def device_of(place, core):
    y, m = place // 3, place % 3
    z = m + jnp.where(m >= y, 1, 0)
    return (y * 4 + z) * 2 + core


def slot_of(place):
    return place // 2 + HEADS * (place % 2)


def sweep_kernel(
    src, rate, ids, w1, b1, w2, b2i, gain, bias, res,
    buf, out, parts, W1, W2, W2b, b2, send_sem, recv_sem, own_sem, pass_sem, res_send, res_recv,
):
    me = greet("tm")
    core, y, z = me % 2, me // 8, me // 2 % 4
    place = y * 3 + z - jnp.where(z > y, 1, 0)
    active = y != z
    is_chain = active & (place % 2 == 0)
    is_attention = active & (place % 2 == 1)
    head = place // 2
    half = me // HALF
    short = pl.ds(0, 256)

    def parcel(r):
        return pltpu.make_async_remote_copy(
            src_ref=src.at[slot_of(r)],
            dst_ref=buf.at[me],
            send_sem=send_sem.at[r],
            recv_sem=recv_sem.at[me],
            device_id={"tm": device_of(r, half)},
            device_id_type=MESH,
        )

    def each(kind, count, act):
        @pl.loop(0, count)
        def _(k):
            r = 2 * k + kind

            @pl.when(device_of(r, half) != me)
            def _():
                act(r)

    @pl.when(active & (core == half))
    def _():
        own = pltpu.make_async_copy(src.at[slot_of(place)], buf.at[me], own_sem)
        own.start()
        own.wait()

    urgent = (me < 8) | (me >= N_TM - 8)
    each(0, jnp.where(urgent, HEADS, 0), lambda r: parcel(r).start())
    each(1, HEADS, lambda r: parcel(r).start())
    each(0, jnp.where(urgent, 0, HEADS), lambda r: parcel(r).start())

    def passing(i, part):
        block = buf.at[i, short] if part else buf.at[i]
        return pltpu.make_async_remote_copy(
            src_ref=block,
            dst_ref=block,
            send_sem=pass_sem.at[i],
            recv_sem=recv_sem.at[i],
            device_id={"tm": me + 1 - 2 * core},
            device_id_type=MESH,
        )

    def landed(i, part):
        direct = i // HALF == core

        @pl.when(direct & (i != me))
        def _():
            pltpu.make_async_copy(buf.at[i], buf.at[i], recv_sem.at[i]).wait()

        @pl.when(direct)
        def _():
            passing(i, part).start()

        @pl.when(jnp.logical_not(direct))
        def _():
            passing(i, part).wait_recv()

    def result(i):
        slot = jnp.where(is_chain, 2 * head + core, CHAINS + head)
        return out.at[i], res.at[slot], res_send.at[i], res_recv.at[slot]

    def away(i):
        block, there, sent, got = result(i)
        return pltpu.make_async_remote_copy(
            src_ref=block,
            dst_ref=there,
            send_sem=sent,
            recv_sem=got,
            device_id={"tm": i},
            device_id_type=MESH,
        )

    def here(i):
        block, there, sent, _ = result(i)
        return pltpu.make_async_copy(block, there, sent)

    def deliver(i):
        @pl.when(i != me)
        def _():
            away(i).start()

        @pl.when(i == me)
        def _():
            here(i).start()

    def delivered(i):
        @pl.when(i != me)
        def _():
            away(i).wait_send()

        @pl.when(i == me)
        def _():
            here(i).wait()

    def passed(part):
        pl.loop(core * HALF, core * HALF + HALF)(lambda i: passing(i, part).wait_send())

    @pl.when(is_chain)
    def _():
        rev = core == 1
        row = pl.ds(head, 1)

        def real(i):
            return jnp.where(rev, N_TM - 1 - i, i)

        chain(
            rev, rate[head], buf, w1[head], b1[row, :], w2[head], b2i[row, :], gain[row, :], bias[row, :],
            out, W1, W2, W2b, b2, lambda i: landed(real(i), False), lambda i: deliver(real(i)),
        )
        passed(False)
        pl.loop(0, N_TM)(delivered)

    @pl.when(is_attention)
    def _():
        pl.loop(core * HALF, core * HALF + HALF)(lambda i: landed(i, True))
        other = (1 - core) * HALF
        pl.loop(other, other + HALF)(lambda i: landed(i, True))
        attend(core, ids, buf, parts, out, deliver)
        passed(True)
        pl.loop(core * HALF, core * HALF + HALF)(delivered)

    each(0, HEADS, lambda r: parcel(r).wait_send())
    each(1, HEADS, lambda r: parcel(r).wait_send())

    @pl.loop(0, 3 * HEADS)
    def _(slot):
        origin = jnp.where(
            slot < CHAINS,
            device_of(slot // 2 * 2, slot % 2),
            device_of((slot - CHAINS) * 2 + 1, half),
        )

        @pl.when(origin != me)
        def _():
            pltpu.make_async_copy(res.at[slot], res.at[slot], res_recv.at[slot]).wait()


def tile_row(ref, g):
    return jnp.concatenate([ref[2 * g : 2 * g + 1, :], ref[2 * g + 1 : 2 * g + 2, :]], 1)


def swap_halves(x):
    return jnp.concatenate([x[:, 64:], x[:, :64]], 1)


def project_kernel(tok, w_hbm, gain, bias, src, qrows, toks, w, acc, send_sem, recv_sem, w_sem):
    me = lax.axis_index("head")
    fetch = pltpu.make_async_copy(w_hbm, w, w_sem)
    fetch.start()
    greet("head")

    def parcel(k):
        return pltpu.make_async_remote_copy(
            src_ref=tok,
            dst_ref=toks.at[me],
            send_sem=send_sem.at[k],
            recv_sem=recv_sem.at[me],
            device_id={"head": lax.rem(me + k, N_HEAD)},
            device_id_type=MESH,
        )

    pl.loop(1, N_HEAD)(lambda k: parcel(k).start())
    fetch.wait()

    def add(x, s, fresh):
        rows = pl.ds(pl.multiple_of(s * WIDTH, WIDTH), WIDTH)
        for c in range(3):
            cols = slice(c * WIDTH, (c + 1) * WIDTH)
            y = mm(x, w[c, rows, :])
            acc[:, cols] = y if fresh else acc[:, cols] + y

    add(tok[...], me, True)

    @pl.loop(1, N_HEAD)
    def _(k):
        s = lax.rem(me + N_HEAD - k, N_HEAD)
        pltpu.make_async_copy(toks.at[s], toks.at[s], recv_sem.at[s]).wait()
        add(toks[s], s, False)

    low = lanes((256, 128)) < 64
    low_half = lanes((128, 128)) < 64
    r = lax.broadcasted_iota(jnp.int32, (128, 128), 0)
    same = jnp.where((r < 64) == low_half, 1.0 / HDIM, 0.0).astype(B)

    def scaled(x):
        sq = x * x
        hi = sq.astype(B)
        return x * lax.rsqrt(mm(hi, same) + mm((sq - hi.astype(F)).astype(B), same) + EPS)

    def pack_rows(left, right):
        pairs = [jnp.where(low, left, swap_halves(right)), jnp.where(low, swap_halves(left), right)]
        return pairs

    def pack_pairs(x):
        y = swap_halves(x)
        even = [jnp.where(low[:64], x[a : a + 64], y[a + 64 : a + 128]) for a in (0, 128)]
        odd = [jnp.where(low[:64], y[a : a + 64], x[a + 64 : a + 128]) for a in (0, 128)]
        return jnp.concatenate(even, 0), jnp.concatenate(odd, 0)

    for g in range(HEADS // 2):
        q, k, v = (
            acc[:, c * WIDTH + g * 128 : c * WIDTH + (g + 1) * 128].astype(B).astype(F) for c in range(3)
        )
        qn, kn, vn = scaled(q), scaled(k), scaled(v)
        qrows[:, g * 128 : (g + 1) * 128] = qn
        aim = (tile_row(bias, g) - (vn - kn)) * tile_row(gain, g)
        sets = ((kn, aim, qn, 0), (k, v, q * HDIM**-0.5, HEADS))
        for left, right, quer, offset in sets:
            tops, tails = pack_rows(left, right), pack_pairs(quer)
            for e in range(2):
                src[offset + 2 * g + e, 0:256, :] = tops[e].astype(B)
                src[offset + 2 * g + e, 256:PACK, :] = tails[e].astype(B)

    pl.loop(1, N_HEAD)(lambda k: parcel(k).wait_send())


def finish_kernel(res, qrows, gate, w, out, mixed, terms, got, send_sem, recv_sem):
    me = greet("head")
    low = lanes((64, 128)) < 64
    for g in range(HEADS // 2):
        weight = jnp.tanh(tile_row(gate, g))
        for p in range(2):
            rows = slice(p * 64, p * 64 + 64)
            both = []
            for e in range(2):
                h = 2 * g + e
                swept = res[2 * h, rows, :].astype(F) + res[2 * h + 1, rows, :].astype(F)
                both.append((swept, res[CHAINS + h, rows, :].astype(F)))
            for c in range(2):
                at = slice((2 * p + c) * 64, (2 * p + c + 1) * 64)
                swept, attention = (
                    jnp.where(low, x, swap_halves(y)) if c == 0 else jnp.where(low, swap_halves(x), y)
                    for x, y in zip(both[0], both[1])
                )
                cols = slice(g * 128, g * 128 + 128)
                mixed[at, cols] = (attention + weight * (swept + 2.0 * qrows[at, cols])).astype(B)

    def part(d):
        cols = pl.ds(pl.multiple_of(d * WIDTH, WIDTH), WIDTH)
        return mm(mixed[...], w[:, cols])

    def parcel(k):
        return pltpu.make_async_remote_copy(
            src_ref=terms.at[k],
            dst_ref=got.at[me],
            send_sem=send_sem.at[k],
            recv_sem=recv_sem.at[me],
            device_id={"head": lax.rem(me + k, N_HEAD)},
            device_id_type=MESH,
        )

    @pl.loop(1, N_HEAD)
    def _(k):
        terms[k] = part(lax.rem(me + k, N_HEAD)).astype(B)
        parcel(k).start()

    def gather(k, total):
        s = lax.rem(me + N_HEAD - k, N_HEAD)
        pltpu.make_async_copy(got.at[s], got.at[s], recv_sem.at[s]).wait()
        return total + got[s].astype(F)

    out[...] = lax.fori_loop(1, N_HEAD, gather, part(me)).astype(B)
    pl.loop(1, N_HEAD)(lambda k: parcel(k).wait_send())


def call(kernel, shapes, memory, scratch, name, collective_id):
    several = len(shapes) > 1
    spaces = {"v": pltpu.VMEM, "s": pltpu.SMEM, "h": pl.ANY}
    ins, outs = memory
    specs = [pl.BlockSpec(memory_space=spaces[m]) for m in outs]
    return pl.pallas_call(
        kernel,
        out_shape=shapes if several else shapes[0],
        in_specs=[pl.BlockSpec(memory_space=spaces[m]) for m in ins],
        out_specs=specs if several else specs[0],
        scratch_shapes=scratch,
        compiler_params=pltpu.CompilerParams(
            collective_id=collective_id, has_side_effects=True, vmem_limit_bytes=48 * 2**20
        ),
        name=name,
    )


def local(
    tokens,
    qkv_weight,
    out_weight,
    segment_ids,
    inner_w1,
    inner_b1,
    inner_w2,
    inner_b2,
    norm_gain,
    norm_bias,
    inner_rate,
    out_gate,
):
    rows = tokens.shape[0]
    dma = pltpu.SemaphoreType.DMA
    src, qrows = call(
        project_kernel,
        [
            jax.ShapeDtypeStruct((2 * HEADS, PACK, 128), B),
            jax.ShapeDtypeStruct((rows, WIDTH), F),
        ],
        ("vhvv", "vv"),
        [
            pltpu.VMEM((N_HEAD, rows, WIDTH), B),
            pltpu.VMEM(qkv_weight.shape, B),
            pltpu.VMEM((rows, 3 * WIDTH), F),
            dma((N_HEAD,)),
            dma((N_HEAD,)),
            dma,
        ],
        "project",
        1,
    )(tokens, qkv_weight, norm_gain, norm_bias)
    res = call(
        sweep_kernel,
        [jax.ShapeDtypeStruct((3 * HEADS, 128, 128), B)],
        ("vss" + "v" * 6, "h"),
        [
            pltpu.VMEM((N_TM, PACK, 128), B),
            pltpu.VMEM((N_TM, 128, 128), B),
            pltpu.VMEM((UNITS, 256, 128), F),
            pltpu.VMEM((128, 256), F),
            pltpu.VMEM((64, 256), F),
            pltpu.VMEM((64, 256), B),
            pltpu.VMEM((1, 128), F),
            dma((PLACES,)),
            dma((N_TM,)),
            dma,
            dma((N_TM,)),
            dma((N_TM,)),
            dma((3 * HEADS,)),
        ],
        "sweep",
        2,
    )(
        src,
        inner_rate,
        segment_ids,
        inner_w1,
        inner_b1,
        inner_w2,
        inner_b2,
        norm_gain,
        norm_bias,
    )
    return call(
        finish_kernel,
        [jax.ShapeDtypeStruct((rows, WIDTH), B)],
        ("vvvv", "v"),
        [
            pltpu.VMEM((rows, WIDTH), B),
            pltpu.VMEM((N_HEAD, rows, WIDTH), B),
            pltpu.VMEM((N_HEAD, rows, WIDTH), B),
            dma((N_HEAD,)),
            dma((N_HEAD,)),
        ],
        "finish",
        3,
    )(res, qrows, out_gate, out_weight)


def solution(mesh):
    placed = (
        P("tm", "head"),
        P(None, None, "head"),
        P("head", None),
        P(),
        P("head", None, None),
        P("head", None),
        P("head", None, None),
        P("head", None),
        P("head", None),
        P("head", None),
        P("head"),
        P("head", None),
    )
    return jax.shard_map(
        local, mesh=mesh, in_specs=placed, out_specs=P("tm", "head"), check_vma=False
    )
```

```python
import jax
import jax.numpy as jnp
from jax import lax
from jax.experimental import pallas as pl
from jax.experimental.pallas import tpu as pltpu
from jax.sharding import PartitionSpec as P

MESH = pl.DeviceIdType.MESH
F = jnp.float32
B = jnp.bfloat16
HDIM = 64
GROUP = 64
EPS = 1e-06
NN = (((1,), (0,)), ((), ()))
NT = (((1,), (1,)), ((), ()))
TN = (((0,), (0,)), ((), ()))
C0 = 0.7978845608028654
C1 = 0.044715
N_TM = 32
HEADS = 6
BLOCKS = 128
PACK = 384
CHAINS = 2 * HEADS
PLACES = 2 * HEADS
HALF = N_TM // 2
WINDOW = 4096 // 256 + 1
UNITS = HALF + 2
FAR = 1 << 20
N_HEAD = 8
WIDTH = HEADS * HDIM


def mm(a, b, dims=NN):
    return lax.dot_general(a, b, dims, preferred_element_type=F)


def gelu_both(x):
    x2 = x * x
    th = jnp.tanh(x * (C0 + (C0 * C1) * x2))
    hp = 0.5 + 0.5 * th
    return x * hp, hp + (hp - hp * hp) * (x * (2 * C0 + (6 * C0 * C1) * x2))


def gelu(x):
    x2 = x * x
    th = jnp.tanh(x * (C0 + (C0 * C1) * x2))
    return x * (0.5 + 0.5 * th)


def mean(x):
    return jnp.mean(x, -1, keepdims=True)


def lanes(shape):
    return lax.broadcasted_iota(jnp.int32, shape, 1)


def chain(rev, rate, buf, w1, b1, w2, b2i, gn, bs, out, W1, W2, W2b, b2, arrived, finished):
    g2 = gn * gn
    s = rate / (GROUP * HDIM)
    lane = lanes((64, 128))
    tail = jnp.where(lane == 64, 1.0, 0.0).astype(B)

    def place(step):
        b = jnp.clip(step, 0, BLOCKS - 1)
        b = jnp.where(rev, BLOCKS - 1 - b, b)
        return b // 4, b % 4

    def load_ka(step):
        i, j = place(step)
        return buf[i, pl.ds(pl.multiple_of(j * 64, 64), 64), :]

    def load_q(step):
        i, j = place(step)
        both = buf[i, pl.ds(pl.multiple_of(256 + (j // 2) * 64, 64), 64), :]
        swapped = jnp.concatenate([both[:, 64:], both[:, :64]], 1)
        return jnp.where(lane < 64, jnp.where(j % 2 == 0, both, swapped), tail)

    def augment(ka):
        return jnp.where(lane < 64, ka, tail)

    arrived(0)
    W1[0:64] = w1
    W1[64:128] = jnp.where(lax.broadcasted_iota(jnp.int32, (64, 256), 0) == 0, b1, 0.0)
    W2[...] = w2 - jnp.mean(w2, 0, keepdims=True)
    W2b[...] = W2[...].astype(B)
    valid = lane < 64
    valid_row = lanes((1, 128)) < 64

    def widen(x):
        return jnp.concatenate([x, jnp.zeros_like(x)], 1)

    def swap(x):
        return jnp.concatenate([x[:, 64:], x[:, :64]], 1)

    def rowsum(x):
        return jnp.sum(x, -1, keepdims=True) * (1.0 / HDIM)

    b2[...] = widen(b2i - mean(b2i))
    gn, bs, g2 = widen(gn), widen(bs), widen(g2)
    first = augment(load_ka(0))
    base0 = mm(first, W1[...].astype(B))
    zero_rows = jnp.zeros((64, 256), B)

    def body(t, carry):
        G1, base, Pt, KTs, Kt, Zlast = carry
        Ab = jnp.where(valid, swap(load_ka(t)), jnp.zeros((64, 128), B))
        A = Ab.astype(F)
        W2t = W2b[...]
        W2z = jnp.concatenate([W2t, zero_rows], 0)
        b2t = b2[...]
        R = mm(jnp.concatenate([Pt, KTs], 0), G1)
        Z1 = base - R[:64]
        W1n = W1[...] - R[64:]
        W1[...] = W1n
        W1b = W1n.astype(B)
        Kn = augment(load_ka(t + 1))
        Y = mm(jnp.concatenate([load_q(t - 1), Kn], 0), W1b)
        Zq = mm(gelu(Y[:64]).astype(B), W2z, NT) + b2t
        X2, dX = gelu_both(Z1)
        X2b = X2.astype(B)
        Z = mm(X2b, W2z, NT) + b2t
        Zg = Z * g2
        mA = rowsum(A)
        S1, S2, S3, S4 = rowsum(Z * Z), rowsum(Zg), rowsum(Z * Zg), rowsum(A * Z)
        inv = lax.rsqrt(S1 + EPS)
        a1 = inv * inv
        a3 = a1 * (a1 * S3 + inv * S4)
        G2 = a1 * Zg + inv * A - a3 * Z - inv * (inv * S2 + mA)
        G2b = G2.astype(B)[:, :64]
        G1n = (mm(G2b, W2t) * dX).astype(B)
        U = mm(G2b, X2b, TN)
        W2n = W2[...] - s * U
        W2b[...] = W2n.astype(B)
        W2[...] = W2n - jnp.mean(W2n, 0, keepdims=True)
        b2n = jnp.where(valid_row, b2t - s * jnp.sum(G2, 0, keepdims=True), 0.0)
        b2[...] = jnp.where(valid_row, b2n - rowsum(b2n), 0.0)
        Pn = (s * mm(Kn, Kt, NT)).astype(B)
        KTn = (s * Kt.astype(F)).T.astype(B)
        z = jnp.where(valid, Zlast - rowsum(Zlast), 0.0)
        o = (z * lax.rsqrt(rowsum(z * z) + EPS) * gn + bs).astype(B)
        i, j = place(t - 2)
        rows = pl.ds(pl.multiple_of((j // 2) * 64, 64), 64)
        out[i, rows, :] = jnp.where(valid == (j % 2 == 0), jnp.where(j % 2 == 0, o, swap(o)), out[i, rows, :])
        return G1n, Y[64:], Pn, KTn, Kn, Zq

    def group(i, carry):
        @pl.when(i + 1 < N_TM)
        def _():
            arrived(i + 1)

        carry = lax.fori_loop(4 * i, 4 * i + 4, body, carry)

        @pl.when(i > 0)
        def _():
            finished(i - 1)

        return carry

    carry = lax.fori_loop(
        0,
        N_TM,
        group,
        (
            jnp.zeros((64, 256), B),
            base0,
            jnp.zeros((64, 64), B),
            jnp.zeros((128, 64), B),
            first,
            jnp.zeros((64, 128), F),
        ),
    )
    lax.fori_loop(BLOCKS, BLOCKS + 2, body, carry)
    finished(N_TM - 1)


def first_at_least(ids, value):
    found = jnp.int32(0)
    for bit in range(13, -1, -1):
        trial = found + (1 << bit)
        last = ids[jnp.minimum(trial, N_TM * 256) - 1]
        found = jnp.where((trial <= N_TM * 256) & (last < value), trial, found)
    return found


def attend(half, ids, buf, parts, out, finished):
    c1, c2 = first_at_least(ids, 1), first_at_least(ids, 2)
    begin = half * HALF
    low = lanes((128, 128)) < 64
    row = lax.broadcasted_iota(jnp.int32, (256, 1), 0)
    inside = (row % 128) // 64 * 128 + (row // 128) * 64 + row % 64

    def segment(pos):
        return jnp.where(pos >= c1, 1, 0) + jnp.where(pos >= c2, 1, 0)

    def edge(number):
        return jnp.where(number <= 0, 0, jnp.where(number == 1, c1, jnp.where(number == 2, c2, FAR)))

    s0 = segment(begin * 256)
    next1, next2 = edge(s0 + 1) // 256, edge(s0 + 2) // 256

    def unit(u, _):
        above = jnp.where(begin + u - 1 >= next1, 1, 0) + jnp.where(begin + u - 2 >= next2, 1, 0)
        i = jnp.clip(begin + u - above, begin, begin + HALF - 1)
        left, right = edge(s0 + above), edge(s0 + above + 1)
        first = jnp.minimum(left // 256, N_TM - WINDOW)
        both = buf[i, 256:PACK, :]
        swapped = jnp.concatenate([both[:, 64:], both[:, :64]], 1)
        zero = jnp.zeros_like(both)
        q = jnp.concatenate([jnp.where(low, both, zero), jnp.where(low, swapped, zero)], 0)
        kv = buf[pl.ds(first, WINDOW), 0:256, :].reshape(WINDOW * 256, 128)
        pos = first * 256 + lanes((1, WINDOW * 256))
        scores = mm(q, kv, NT) + jnp.where((pos >= left) & (pos < right), 0.0, -1e30)
        w = jnp.exp(scores - jnp.max(scores, -1, keepdims=True))
        total = jnp.sum(w, -1, keepdims=True)
        parts[u] = mm(w.astype(B), kv) / total
        return 0

    lax.fori_loop(0, UNITS, unit, 0)

    def assemble(i, _):
        s1 = segment(i * 256)
        mine = segment(i * 256 + inside) - s1
        u = i - begin + s1 - s0
        o = jnp.where(
            mine == 0,
            parts[jnp.minimum(u, UNITS - 1)],
            jnp.where(
                mine == 1, parts[jnp.minimum(u + 1, UNITS - 1)], parts[jnp.minimum(u + 2, UNITS - 1)]
            ),
        )
        lo = jnp.concatenate([o[:128, 64:], o[:128, :64]], 1)
        out[i] = jnp.where(low, lo, o[128:]).astype(B)
        finished(i)
        return 0

    lax.fori_loop(begin, begin + HALF, assemble, 0)


def greet():
    barrier = pltpu.get_barrier_semaphore()
    for axis, n in (("head", N_HEAD), ("tm", N_TM)):
        me = lax.axis_index(axis)

        @pl.loop(1, n)
        def _(k):
            pl.semaphore_signal(
                barrier, inc=1, device_id={axis: lax.rem(me + k, n)}, device_id_type=MESH
            )

    pl.semaphore_wait(barrier, N_HEAD + N_TM - 2)


def device_of(place, core):
    y, m = place // 3, place % 3
    z = m + jnp.where(m >= y, 1, 0)
    return (y * 4 + z) * 2 + core


def slot_of(place):
    return place // 2 + HEADS * (place % 2)


def layer_kernel(
    tok, w_hbm, wo_hbm, rate, ids, w1, b1, w2, b2i, gain, bias, gate, final,
    toks, w, acc, src, qrows, wo, buf, out, parts, W1, W2, W2b, b2, res, mixed, terms, got,
    tok_send, tok_recv, w_sem, wo_sem, send_sem, recv_sem, own_sem, pass_sem, res_send, res_recv,
    term_send, term_recv,
):
    fetch = pltpu.make_async_copy(w_hbm, w, w_sem)
    fetch.start()
    fetch_out = pltpu.make_async_copy(wo_hbm, wo, wo_sem)
    fetch_out.start()
    greet()
    me = lax.axis_index("tm")
    core, y, z = me % 2, me // 8, me // 2 % 4
    place = y * 3 + z - jnp.where(z > y, 1, 0)
    active = y != z
    is_chain = active & (place % 2 == 0)
    is_attention = active & (place % 2 == 1)
    head = place // 2
    half = me // HALF
    short = pl.ds(0, 256)

    def parcel(r):
        return pltpu.make_async_remote_copy(
            src_ref=src.at[slot_of(r)],
            dst_ref=buf.at[me],
            send_sem=send_sem.at[r],
            recv_sem=recv_sem.at[me],
            device_id={"tm": device_of(r, half)},
            device_id_type=MESH,
        )

    def each(kind, count, act):
        @pl.loop(0, count)
        def _(k):
            r = 2 * k + kind

            @pl.when(device_of(r, half) != me)
            def _():
                act(r)

    def dispatch(kind, head_of):
        r = 2 * head_of + kind

        @pl.when(device_of(r, half) != me)
        def _():
            parcel(r).start()

    sent_tokens = project(
        tok, gain, bias, fetch, src, qrows, toks, w, acc, tok_send, tok_recv, dispatch
    )

    @pl.when(active & (core == half))
    def _():
        own = pltpu.make_async_copy(src.at[slot_of(place)], buf.at[me], own_sem)
        own.start()
        own.wait()

    def passing(i, part):
        block = buf.at[i, short] if part else buf.at[i]
        return pltpu.make_async_remote_copy(
            src_ref=block,
            dst_ref=block,
            send_sem=pass_sem.at[i],
            recv_sem=recv_sem.at[i],
            device_id={"tm": me + 1 - 2 * core},
            device_id_type=MESH,
        )

    def landed(i, part):
        direct = i // HALF == core

        @pl.when(direct & (i != me))
        def _():
            pltpu.make_async_copy(buf.at[i], buf.at[i], recv_sem.at[i]).wait()

        @pl.when(direct)
        def _():
            passing(i, part).start()

        @pl.when(jnp.logical_not(direct))
        def _():
            passing(i, part).wait_recv()

    def result(i):
        slot = jnp.where(is_chain, 2 * head + core, CHAINS + head)
        return out.at[i], res.at[slot], res_send.at[i], res_recv.at[slot]

    def away(i):
        block, there, sent, got = result(i)
        return pltpu.make_async_remote_copy(
            src_ref=block,
            dst_ref=there,
            send_sem=sent,
            recv_sem=got,
            device_id={"tm": i},
            device_id_type=MESH,
        )

    def here(i):
        block, there, sent, _ = result(i)
        return pltpu.make_async_copy(block, there, sent)

    def deliver(i):
        @pl.when(i != me)
        def _():
            away(i).start()

        @pl.when(i == me)
        def _():
            here(i).start()

    def delivered(i):
        @pl.when(i != me)
        def _():
            away(i).wait_send()

        @pl.when(i == me)
        def _():
            here(i).wait()

    def passed(part):
        pl.loop(core * HALF, core * HALF + HALF)(lambda i: passing(i, part).wait_send())

    @pl.when(is_chain)
    def _():
        rev = core == 1
        row = pl.ds(head, 1)

        def real(i):
            return jnp.where(rev, N_TM - 1 - i, i)

        chain(
            rev, rate[head], buf, w1[head], b1[row, :], w2[head], b2i[row, :], gain[row, :], bias[row, :],
            out, W1, W2, W2b, b2, lambda i: landed(real(i), False), lambda i: deliver(real(i)),
        )
        passed(False)
        pl.loop(0, N_TM)(delivered)

    @pl.when(is_attention)
    def _():
        pl.loop(core * HALF, core * HALF + HALF)(lambda i: landed(i, True))
        other = (1 - core) * HALF
        pl.loop(other, other + HALF)(lambda i: landed(i, True))
        attend(core, ids, buf, parts, out, deliver)
        passed(True)
        pl.loop(core * HALF, core * HALF + HALF)(delivered)


    @pl.loop(0, 3 * HEADS)
    def _(slot):
        origin = jnp.where(
            slot < CHAINS,
            device_of(slot // 2 * 2, slot % 2),
            device_of((slot - CHAINS) * 2 + 1, half),
        )

        @pl.when(origin != me)
        def _():
            pltpu.make_async_copy(res.at[slot], res.at[slot], res_recv.at[slot]).wait()

    fetch_out.wait()
    finish(res, qrows, gate, wo, final, mixed, terms, got, term_send, term_recv)
    each(0, HEADS, lambda r: parcel(r).wait_send())
    each(1, HEADS, lambda r: parcel(r).wait_send())
    sent_tokens()


def tile_row(ref, g):
    return jnp.concatenate([ref[2 * g : 2 * g + 1, :], ref[2 * g + 1 : 2 * g + 2, :]], 1)


def swap_halves(x):
    return jnp.concatenate([x[:, 64:], x[:, :64]], 1)


def project(tok, gain, bias, fetch, src, qrows, toks, w, acc, send_sem, recv_sem, dispatch):
    me = lax.axis_index("head")

    def parcel(k):
        return pltpu.make_async_remote_copy(
            src_ref=tok,
            dst_ref=toks.at[me],
            send_sem=send_sem.at[k],
            recv_sem=recv_sem.at[me],
            device_id={"head": lax.rem(me + k, N_HEAD)},
            device_id_type=MESH,
        )

    pl.loop(1, N_HEAD)(lambda k: parcel(k).start())
    fetch.wait()

    def add(x, s, fresh):
        rows = pl.ds(pl.multiple_of(s * WIDTH, WIDTH), WIDTH)
        for c in range(3):
            cols = slice(c * WIDTH, (c + 1) * WIDTH)
            y = mm(x, w[c, rows, :])
            acc[:, cols] = y if fresh else acc[:, cols] + y

    add(tok[...], me, True)

    @pl.loop(1, N_HEAD)
    def _(k):
        s = lax.rem(me + N_HEAD - k, N_HEAD)
        pltpu.make_async_copy(toks.at[s], toks.at[s], recv_sem.at[s]).wait()
        add(toks[s], s, False)

    low = lanes((256, 128)) < 64
    low_half = lanes((128, 128)) < 64
    r = lax.broadcasted_iota(jnp.int32, (128, 128), 0)
    same = jnp.where((r < 64) == low_half, 1.0 / HDIM, 0.0).astype(B)

    def scaled(x):
        sq = x * x
        hi = sq.astype(B)
        return x * lax.rsqrt(mm(hi, same) + mm((sq - hi.astype(F)).astype(B), same) + EPS)

    def pack_rows(left, right):
        pairs = [jnp.where(low, left, swap_halves(right)), jnp.where(low, swap_halves(left), right)]
        return pairs

    def pack_pairs(x):
        y = swap_halves(x)
        even = [jnp.where(low[:64], x[a : a + 64], y[a + 64 : a + 128]) for a in (0, 128)]
        odd = [jnp.where(low[:64], y[a : a + 64], x[a + 64 : a + 128]) for a in (0, 128)]
        return jnp.concatenate(even, 0), jnp.concatenate(odd, 0)

    def pack(g, left, right, quer, kind):
        tops, tails = pack_rows(left, right), pack_pairs(quer)
        for e in range(2):
            slot = HEADS * kind + 2 * g + e
            src[slot, 0:256, :] = tops[e].astype(B)
            src[slot, 256:PACK, :] = tails[e].astype(B)
            dispatch(kind, 2 * g + e)

    def raw(g):
        return (
            acc[:, c * WIDTH + g * 128 : c * WIDTH + (g + 1) * 128].astype(B).astype(F) for c in range(3)
        )

    for g in range(HEADS // 2):
        qn, kn, vn = (scaled(x) for x in raw(g))
        qrows[:, g * 128 : (g + 1) * 128] = qn
        pack(g, kn, (tile_row(bias, g) - (vn - kn)) * tile_row(gain, g), qn, 0)
    for g in range(HEADS // 2):
        q, k, v = raw(g)
        pack(g, k, v, q * HDIM**-0.5, 1)

    return lambda: pl.loop(1, N_HEAD)(lambda k: parcel(k).wait_send())


def finish(res, qrows, gate, w, out, mixed, terms, got, send_sem, recv_sem):
    me = lax.axis_index("head")
    low = lanes((64, 128)) < 64
    for g in range(HEADS // 2):
        weight = jnp.tanh(tile_row(gate, g))
        for p in range(2):
            rows = slice(p * 64, p * 64 + 64)
            both = []
            for e in range(2):
                h = 2 * g + e
                swept = res[2 * h, rows, :].astype(F) + res[2 * h + 1, rows, :].astype(F)
                both.append((swept, res[CHAINS + h, rows, :].astype(F)))
            for c in range(2):
                at = slice((2 * p + c) * 64, (2 * p + c + 1) * 64)
                swept, attention = (
                    jnp.where(low, x, swap_halves(y)) if c == 0 else jnp.where(low, swap_halves(x), y)
                    for x, y in zip(both[0], both[1])
                )
                cols = slice(g * 128, g * 128 + 128)
                mixed[at, cols] = (attention + weight * (swept + 2.0 * qrows[at, cols])).astype(B)

    def part(d):
        cols = pl.ds(pl.multiple_of(d * WIDTH, WIDTH), WIDTH)
        return mm(mixed[...], w[:, cols])

    def parcel(k):
        return pltpu.make_async_remote_copy(
            src_ref=terms.at[k],
            dst_ref=got.at[me],
            send_sem=send_sem.at[k],
            recv_sem=recv_sem.at[me],
            device_id={"head": lax.rem(me + k, N_HEAD)},
            device_id_type=MESH,
        )

    @pl.loop(1, N_HEAD)
    def _(k):
        terms[k] = part(lax.rem(me + k, N_HEAD)).astype(B)
        parcel(k).start()

    def gather(k, total):
        s = lax.rem(me + N_HEAD - k, N_HEAD)
        pltpu.make_async_copy(got.at[s], got.at[s], recv_sem.at[s]).wait()
        return total + got[s].astype(F)

    out[...] = lax.fori_loop(1, N_HEAD, gather, part(me)).astype(B)
    pl.loop(1, N_HEAD)(lambda k: parcel(k).wait_send())


def local(
    tokens,
    qkv_weight,
    out_weight,
    segment_ids,
    inner_w1,
    inner_b1,
    inner_w2,
    inner_b2,
    norm_gain,
    norm_bias,
    inner_rate,
    out_gate,
):
    rows = tokens.shape[0]
    dma = pltpu.SemaphoreType.DMA
    vm, sm, hbm = (pl.BlockSpec(memory_space=m) for m in (pltpu.VMEM, pltpu.SMEM, pl.ANY))
    return pl.pallas_call(
        layer_kernel,
        out_shape=jax.ShapeDtypeStruct((rows, WIDTH), B),
        in_specs=[vm, hbm, hbm, sm, sm] + [vm] * 7,
        out_specs=vm,
        scratch_shapes=[
            pltpu.VMEM((N_HEAD, rows, WIDTH), B),
            pltpu.VMEM(qkv_weight.shape, B),
            pltpu.VMEM((rows, 3 * WIDTH), F),
            pltpu.VMEM((2 * HEADS, PACK, 128), B),
            pltpu.VMEM((rows, WIDTH), F),
            pltpu.VMEM(out_weight.shape, B),
            pltpu.VMEM((N_TM, PACK, 128), B),
            pltpu.VMEM((N_TM, 128, 128), B),
            pltpu.VMEM((UNITS, 256, 128), F),
            pltpu.VMEM((128, 256), F),
            pltpu.VMEM((64, 256), F),
            pltpu.VMEM((64, 256), B),
            pltpu.VMEM((1, 128), F),
            pltpu.VMEM((3 * HEADS, 128, 128), B),
            pltpu.VMEM((rows, WIDTH), B),
            pltpu.VMEM((N_HEAD, rows, WIDTH), B),
            pltpu.VMEM((N_HEAD, rows, WIDTH), B),
            dma((N_HEAD,)),
            dma((N_HEAD,)),
            dma,
            dma,
            dma((PLACES,)),
            dma((N_TM,)),
            dma,
            dma((N_TM,)),
            dma((N_TM,)),
            dma((3 * HEADS,)),
            dma((N_HEAD,)),
            dma((N_HEAD,)),
        ],
        compiler_params=pltpu.CompilerParams(
            collective_id=1, has_side_effects=True, vmem_limit_bytes=56 * 2**20
        ),
        name="layer",
    )(
        tokens,
        qkv_weight,
        out_weight,
        inner_rate,
        segment_ids,
        inner_w1,
        inner_b1,
        jnp.swapaxes(inner_w2, 1, 2),
        inner_b2,
        norm_gain,
        norm_bias,
        out_gate,
    )


def solution(mesh):
    placed = (
        P("tm", "head"),
        P(None, None, "head"),
        P("head", None),
        P(),
        P("head", None, None),
        P("head", None),
        P("head", None, None),
        P("head", None),
        P("head", None),
        P("head", None),
        P("head"),
        P("head", None),
    )
    return jax.shard_map(
        local, mesh=mesh, in_specs=placed, out_specs=P("tm", "head"), check_vma=False
    )
```

```python
import jax
import jax.numpy as jnp
from jax import lax
from jax.experimental import pallas as pl
from jax.experimental.pallas import tpu as pltpu
from jax.sharding import PartitionSpec as P

MESH = pl.DeviceIdType.MESH
F = jnp.float32
B = jnp.bfloat16
HDIM = 64
GROUP = 64
EPS = 1e-06
NN = (((1,), (0,)), ((), ()))
NT = (((1,), (1,)), ((), ()))
TN = (((0,), (0,)), ((), ()))
C0 = 0.7978845608028654
C1 = 0.044715
N_TM = 32
HEADS = 6
BLOCKS = 128
PACK = 384
CHAINS = 2 * HEADS
PLACES = 2 * HEADS
HALF = N_TM // 2
WINDOW = 4096 // 256 + 1
UNITS = HALF + 2
FAR = 1 << 20
N_HEAD = 8
WIDTH = HEADS * HDIM


def mm(a, b, dims=NN):
    return lax.dot_general(a, b, dims, preferred_element_type=F)


def gelu_both(x):
    x2 = x * x
    th = jnp.tanh(x * (C0 + (C0 * C1) * x2))
    hp = 0.5 + 0.5 * th
    return x * hp, hp + (hp - hp * hp) * (x * (2 * C0 + (6 * C0 * C1) * x2))


def gelu(x):
    x2 = x * x
    th = jnp.tanh(x * (C0 + (C0 * C1) * x2))
    return x * (0.5 + 0.5 * th)


def mean(x):
    return jnp.mean(x, -1, keepdims=True)


def lanes(shape):
    return lax.broadcasted_iota(jnp.int32, shape, 1)


def chain(rev, rate, buf, w1, b1, w2, b2i, gn, bs, out, W1, W2, W2b, b2, arrived, finished):
    g2 = gn * gn
    s = rate / (GROUP * HDIM)
    lane = lanes((64, 128))
    tail = jnp.where(lane == 64, 1.0, 0.0).astype(B)

    def place(step):
        b = jnp.clip(step, 0, BLOCKS - 1)
        b = jnp.where(rev, BLOCKS - 1 - b, b)
        return b // 4, b % 4

    def load_ka(step):
        i, j = place(step)
        return buf[i, pl.ds(pl.multiple_of(j * 64, 64), 64), :]

    def load_q(step):
        i, j = place(step)
        both = buf[i, pl.ds(pl.multiple_of(256 + (j // 2) * 64, 64), 64), :]
        swapped = jnp.concatenate([both[:, 64:], both[:, :64]], 1)
        return jnp.where(lane < 64, jnp.where(j % 2 == 0, both, swapped), tail)

    def augment(ka):
        return jnp.where(lane < 64, ka, tail)

    arrived(0)
    W1[0:64] = w1
    W1[64:128] = jnp.where(lax.broadcasted_iota(jnp.int32, (64, 256), 0) == 0, b1, 0.0)
    W2[...] = w2 - jnp.mean(w2, 0, keepdims=True)
    W2b[...] = W2[...].astype(B)
    valid = lane < 64
    valid_row = lanes((1, 128)) < 64

    def widen(x):
        return jnp.concatenate([x, jnp.zeros_like(x)], 1)

    def swap(x):
        return jnp.concatenate([x[:, 64:], x[:, :64]], 1)

    def rowsum(x):
        return jnp.sum(x, -1, keepdims=True) * (1.0 / HDIM)

    b2[...] = widen(b2i - mean(b2i))
    gn, bs, g2 = widen(gn), widen(bs), widen(g2)
    first = augment(load_ka(0))
    base0 = mm(first, W1[...].astype(B))
    zero_rows = jnp.zeros((64, 256), B)

    def body(t, carry):
        G1, base, Pt, KTs, Kt, Zlast = carry
        Ab = jnp.where(valid, swap(load_ka(t)), jnp.zeros((64, 128), B))
        A = Ab.astype(F)
        W2t = W2b[...]
        W2z = jnp.concatenate([W2t, zero_rows], 0)
        b2t = b2[...]
        R = mm(jnp.concatenate([Pt, KTs], 0), G1)
        Z1 = base - R[:64]
        W1n = W1[...] - R[64:]
        W1[...] = W1n
        W1b = W1n.astype(B)
        Kn = augment(load_ka(t + 1))
        Y = mm(jnp.concatenate([load_q(t - 1), Kn], 0), W1b)
        Zq = mm(gelu(Y[:64]).astype(B), W2z, NT) + b2t
        X2, dX = gelu_both(Z1)
        X2b = X2.astype(B)
        Z = mm(X2b, W2z, NT) + b2t
        Zg = Z * g2
        S1, S3, S4 = rowsum(Z * Z), rowsum(Z * Zg), rowsum(A * Z)
        inv = lax.rsqrt(S1 + EPS)
        a1 = inv * inv
        a3 = a1 * (a1 * S3 + inv * S4)
        G2 = a1 * Zg + inv * A - a3 * Z
        G2b = G2.astype(B)[:, :64]
        G1n = (mm(G2b, W2t) * dX).astype(B)
        U = mm(G2b, X2b, TN)
        W2n = W2[...] - s * U
        W2n = W2n - jnp.mean(W2n, 0, keepdims=True)
        W2b[...] = W2n.astype(B)
        W2[...] = W2n
        b2n = jnp.where(valid_row, b2t - s * jnp.sum(G2, 0, keepdims=True), 0.0)
        b2[...] = jnp.where(valid_row, b2n - rowsum(b2n), 0.0)
        Pn = (s * mm(Kn, Kt, NT)).astype(B)
        KTn = (s * Kt.astype(F)).T.astype(B)
        z = jnp.where(valid, Zlast - rowsum(Zlast), 0.0)
        o = (z * lax.rsqrt(rowsum(z * z) + EPS) * gn + bs).astype(B)
        i, j = place(t - 2)
        rows = pl.ds(pl.multiple_of((j // 2) * 64, 64), 64)
        out[i, rows, :] = jnp.where(valid == (j % 2 == 0), jnp.where(j % 2 == 0, o, swap(o)), out[i, rows, :])
        return G1n, Y[64:], Pn, KTn, Kn, Zq

    def group(i, carry):
        @pl.when(i + 1 < N_TM)
        def _():
            arrived(i + 1)

        carry = lax.fori_loop(4 * i, 4 * i + 4, body, carry)

        @pl.when(i > 0)
        def _():
            finished(i - 1)

        return carry

    carry = lax.fori_loop(
        0,
        N_TM,
        group,
        (
            jnp.zeros((64, 256), B),
            base0,
            jnp.zeros((64, 64), B),
            jnp.zeros((128, 64), B),
            first,
            jnp.zeros((64, 128), F),
        ),
    )
    lax.fori_loop(BLOCKS, BLOCKS + 2, body, carry)
    finished(N_TM - 1)


def first_at_least(ids, value):
    found = jnp.int32(0)
    for bit in range(13, -1, -1):
        trial = found + (1 << bit)
        last = ids[jnp.minimum(trial, N_TM * 256) - 1]
        found = jnp.where((trial <= N_TM * 256) & (last < value), trial, found)
    return found


def attend(half, ids, buf, parts, out, finished):
    c1, c2 = first_at_least(ids, 1), first_at_least(ids, 2)
    begin = half * HALF
    low = lanes((128, 128)) < 64
    row = lax.broadcasted_iota(jnp.int32, (256, 1), 0)
    inside = (row % 128) // 64 * 128 + (row // 128) * 64 + row % 64

    def segment(pos):
        return jnp.where(pos >= c1, 1, 0) + jnp.where(pos >= c2, 1, 0)

    def edge(number):
        return jnp.where(number <= 0, 0, jnp.where(number == 1, c1, jnp.where(number == 2, c2, FAR)))

    s0 = segment(begin * 256)
    next1, next2 = edge(s0 + 1) // 256, edge(s0 + 2) // 256

    def unit(u, _):
        above = jnp.where(begin + u - 1 >= next1, 1, 0) + jnp.where(begin + u - 2 >= next2, 1, 0)
        i = jnp.clip(begin + u - above, begin, begin + HALF - 1)
        left, right = edge(s0 + above), edge(s0 + above + 1)
        first = jnp.minimum(left // 256, N_TM - WINDOW)
        both = buf[i, 256:PACK, :]
        swapped = jnp.concatenate([both[:, 64:], both[:, :64]], 1)
        zero = jnp.zeros_like(both)
        q = jnp.concatenate([jnp.where(low, both, zero), jnp.where(low, swapped, zero)], 0)
        kv = buf[pl.ds(first, WINDOW), 0:256, :].reshape(WINDOW * 256, 128)
        pos = first * 256 + lanes((1, WINDOW * 256))
        scores = mm(q, kv, NT) + jnp.where((pos >= left) & (pos < right), 0.0, -1e30)
        w = jnp.exp(scores - jnp.max(scores, -1, keepdims=True))
        total = jnp.sum(w, -1, keepdims=True)
        parts[u] = mm(w.astype(B), kv) / total
        return 0

    lax.fori_loop(0, UNITS, unit, 0)

    def assemble(i, _):
        s1 = segment(i * 256)
        mine = segment(i * 256 + inside) - s1
        u = i - begin + s1 - s0
        o = jnp.where(
            mine == 0,
            parts[jnp.minimum(u, UNITS - 1)],
            jnp.where(
                mine == 1, parts[jnp.minimum(u + 1, UNITS - 1)], parts[jnp.minimum(u + 2, UNITS - 1)]
            ),
        )
        lo = jnp.concatenate([o[:128, 64:], o[:128, :64]], 1)
        out[i] = jnp.where(low, lo, o[128:]).astype(B)
        finished(i)
        return 0

    lax.fori_loop(begin, begin + HALF, assemble, 0)


def greet():
    barrier = pltpu.get_barrier_semaphore()
    for axis, n in (("head", N_HEAD), ("tm", N_TM)):
        me = lax.axis_index(axis)

        @pl.loop(1, n)
        def _(k):
            pl.semaphore_signal(
                barrier, inc=1, device_id={axis: lax.rem(me + k, n)}, device_id_type=MESH
            )

    pl.semaphore_wait(barrier, N_HEAD + N_TM - 2)


def device_of(place, core):
    y, m = place // 3, place % 3
    z = m + jnp.where(m >= y, 1, 0)
    return (y * 4 + z) * 2 + core


def slot_of(place):
    return place // 2 + HEADS * (place % 2)


def layer_kernel(
    tok, w_hbm, wo_hbm, rate, ids, w1, b1, w2, b2i, gain, bias, gate, final,
    toks, w, acc, src, qrows, wo, buf, out, parts, W1, W2, W2b, b2, res, mixed, terms, got,
    tok_send, tok_recv, w_sem, wo_sem, send_sem, recv_sem, own_sem, pass_sem, res_send, res_recv,
    term_send, term_recv,
):
    fetch = pltpu.make_async_copy(w_hbm, w, w_sem)
    fetch.start()
    fetch_out = pltpu.make_async_copy(wo_hbm, wo, wo_sem)
    fetch_out.start()
    greet()
    me = lax.axis_index("tm")
    core, y, z = me % 2, me // 8, me // 2 % 4
    place = y * 3 + z - jnp.where(z > y, 1, 0)
    active = y != z
    is_chain = active & (place % 2 == 0)
    is_attention = active & (place % 2 == 1)
    head = place // 2
    half = me // HALF
    short = pl.ds(0, 256)

    def parcel(r):
        return pltpu.make_async_remote_copy(
            src_ref=src.at[slot_of(r)],
            dst_ref=buf.at[me],
            send_sem=send_sem.at[r],
            recv_sem=recv_sem.at[me],
            device_id={"tm": device_of(r, half)},
            device_id_type=MESH,
        )

    def each(kind, count, act):
        @pl.loop(0, count)
        def _(k):
            r = 2 * k + kind

            @pl.when(device_of(r, half) != me)
            def _():
                act(r)

    def dispatch(kind, head_of):
        r = 2 * head_of + kind

        @pl.when(device_of(r, half) != me)
        def _():
            parcel(r).start()

    sent_tokens = project(
        tok, gain, bias, fetch, src, qrows, toks, w, acc, tok_send, tok_recv, dispatch
    )

    @pl.when(active & (core == half))
    def _():
        own = pltpu.make_async_copy(src.at[slot_of(place)], buf.at[me], own_sem)
        own.start()
        own.wait()

    def passing(i, part):
        block = buf.at[i, short] if part else buf.at[i]
        return pltpu.make_async_remote_copy(
            src_ref=block,
            dst_ref=block,
            send_sem=pass_sem.at[i],
            recv_sem=recv_sem.at[i],
            device_id={"tm": me + 1 - 2 * core},
            device_id_type=MESH,
        )

    def landed(i, part):
        direct = i // HALF == core

        @pl.when(direct & (i != me))
        def _():
            pltpu.make_async_copy(buf.at[i], buf.at[i], recv_sem.at[i]).wait()

        @pl.when(direct)
        def _():
            passing(i, part).start()

        @pl.when(jnp.logical_not(direct))
        def _():
            passing(i, part).wait_recv()

    def result(i):
        slot = jnp.where(is_chain, 2 * head + core, CHAINS + head)
        return out.at[i], res.at[slot], res_send.at[i], res_recv.at[slot]

    def away(i):
        block, there, sent, got = result(i)
        return pltpu.make_async_remote_copy(
            src_ref=block,
            dst_ref=there,
            send_sem=sent,
            recv_sem=got,
            device_id={"tm": i},
            device_id_type=MESH,
        )

    def here(i):
        block, there, sent, _ = result(i)
        return pltpu.make_async_copy(block, there, sent)

    def deliver(i):
        @pl.when(i != me)
        def _():
            away(i).start()

        @pl.when(i == me)
        def _():
            here(i).start()

    def delivered(i):
        @pl.when(i != me)
        def _():
            away(i).wait_send()

        @pl.when(i == me)
        def _():
            here(i).wait()

    def passed(part):
        pl.loop(core * HALF, core * HALF + HALF)(lambda i: passing(i, part).wait_send())

    @pl.when(is_chain)
    def _():
        rev = core == 1
        row = pl.ds(head, 1)

        def real(i):
            return jnp.where(rev, N_TM - 1 - i, i)

        chain(
            rev, rate[head], buf, w1[head], b1[row, :], w2[head], b2i[row, :], gain[row, :], bias[row, :],
            out, W1, W2, W2b, b2, lambda i: landed(real(i), False), lambda i: deliver(real(i)),
        )
        passed(False)
        pl.loop(0, N_TM)(delivered)

    @pl.when(is_attention)
    def _():
        pl.loop(core * HALF, core * HALF + HALF)(lambda i: landed(i, True))
        other = (1 - core) * HALF
        pl.loop(other, other + HALF)(lambda i: landed(i, True))
        attend(core, ids, buf, parts, out, deliver)
        passed(True)
        pl.loop(core * HALF, core * HALF + HALF)(delivered)


    @pl.loop(0, 3 * HEADS)
    def _(slot):
        origin = jnp.where(
            slot < CHAINS,
            device_of(slot // 2 * 2, slot % 2),
            device_of((slot - CHAINS) * 2 + 1, half),
        )

        @pl.when(origin != me)
        def _():
            pltpu.make_async_copy(res.at[slot], res.at[slot], res_recv.at[slot]).wait()

    fetch_out.wait()
    finish(res, qrows, gate, wo, final, mixed, terms, got, term_send, term_recv)
    each(0, HEADS, lambda r: parcel(r).wait_send())
    each(1, HEADS, lambda r: parcel(r).wait_send())
    sent_tokens()


def tile_row(ref, g):
    return jnp.concatenate([ref[2 * g : 2 * g + 1, :], ref[2 * g + 1 : 2 * g + 2, :]], 1)


def swap_halves(x):
    return jnp.concatenate([x[:, 64:], x[:, :64]], 1)


def project(tok, gain, bias, fetch, src, qrows, toks, w, acc, send_sem, recv_sem, dispatch):
    me = lax.axis_index("head")

    def add(x, s, fresh):
        rows = pl.ds(pl.multiple_of(s * WIDTH, WIDTH), WIDTH)
        for c in range(3):
            cols = slice(c * WIDTH, (c + 1) * WIDTH)
            y = mm(x, w[c, rows, :])
            acc[:, cols] = y if fresh else acc[:, cols] + y

    level, x = me // 4, me % 4

    def at(other, step):
        z = 1 - level if other else level
        return z * 4 + (x + step) % 4

    right, left, across = at(0, 1), at(0, 3), at(1, 0)
    sends = []

    def push(block, s, dest, part=None):
        rows = pl.ds(0, 256) if part is None else pl.ds(128 * part, 128)
        copy = pltpu.make_async_remote_copy(
            src_ref=block.at[rows],
            dst_ref=toks.at[s, rows],
            send_sem=send_sem.at[len(sends)],
            recv_sem=recv_sem.at[s, part or 0],
            device_id={"head": dest},
            device_id_type=MESH,
        )
        copy.start()
        sends.append(copy)

    def take(s, halves=False):
        for part in range(2 if halves else 1):
            rows = pl.ds(128 * part, 128) if halves else pl.ds(0, 256)
            piece = toks.at[s, rows]
            pltpu.make_async_copy(piece, piece, recv_sem.at[s, part]).wait()

    for dest in (across, right, left):
        push(tok, me, dest)
    fetch.wait()
    add(tok[...], me, True)
    take(across)
    push(toks.at[across], across, right)
    push(toks.at[across], across, left)
    for other in (0, 1):
        for step, dest, part in ((3, right, 0), (1, left, 1)):
            s = at(other, step)
            take(s)
            push(toks.at[s], s, dest, part)
            if not other and step == 3:
                add(toks[across], across, False)
            add(toks[s], s, False)
    for other in (0, 1):
        take(at(other, 2), True)
        add(toks[at(other, 2)], at(other, 2), False)

    low = lanes((256, 128)) < 64
    low_half = lanes((128, 128)) < 64
    r = lax.broadcasted_iota(jnp.int32, (128, 128), 0)
    same = jnp.where((r < 64) == low_half, 1.0 / HDIM, 0.0).astype(B)

    def group_mean(x):
        hi = x.astype(B)
        return mm(hi, same) + mm((x - hi.astype(F)).astype(B), same)

    def scaled(x):
        return x * lax.rsqrt(group_mean(x * x) + EPS)

    def pack_rows(left, right):
        pairs = [jnp.where(low, left, swap_halves(right)), jnp.where(low, swap_halves(left), right)]
        return pairs

    def pack_pairs(x):
        y = swap_halves(x)
        even = [jnp.where(low[:64], x[a : a + 64], y[a + 64 : a + 128]) for a in (0, 128)]
        odd = [jnp.where(low[:64], y[a : a + 64], x[a + 64 : a + 128]) for a in (0, 128)]
        return jnp.concatenate(even, 0), jnp.concatenate(odd, 0)

    def pack(g, left, right, quer, kind):
        tops, tails = pack_rows(left, right), pack_pairs(quer)
        for e in range(2):
            slot = HEADS * kind + 2 * g + e
            src[slot, 0:256, :] = tops[e].astype(B)
            src[slot, 256:PACK, :] = tails[e].astype(B)
            dispatch(kind, 2 * g + e)

    def raw(g):
        return (
            acc[:, c * WIDTH + g * 128 : c * WIDTH + (g + 1) * 128].astype(B).astype(F) for c in range(3)
        )

    for g in range(HEADS // 2):
        qn, kn, vn = (scaled(x) for x in raw(g))
        qrows[:, g * 128 : (g + 1) * 128] = qn
        aim = (tile_row(bias, g) - (vn - kn)) * tile_row(gain, g)
        pack(g, kn, aim - group_mean(aim), qn, 0)
    for g in range(HEADS // 2):
        q, k, v = raw(g)
        pack(g, k, v, q * HDIM**-0.5, 1)

    def sent():
        for copy in sends:
            copy.wait_send()

    return sent


def finish(res, qrows, gate, w, out, mixed, terms, got, send_sem, recv_sem):
    me = lax.axis_index("head")
    low = lanes((64, 128)) < 64
    for g in range(HEADS // 2):
        weight = jnp.tanh(tile_row(gate, g))
        for p in range(2):
            rows = slice(p * 64, p * 64 + 64)
            both = []
            for e in range(2):
                h = 2 * g + e
                swept = res[2 * h, rows, :].astype(F) + res[2 * h + 1, rows, :].astype(F)
                both.append((swept, res[CHAINS + h, rows, :].astype(F)))
            for c in range(2):
                at = slice((2 * p + c) * 64, (2 * p + c + 1) * 64)
                swept, attention = (
                    jnp.where(low, x, swap_halves(y)) if c == 0 else jnp.where(low, swap_halves(x), y)
                    for x, y in zip(both[0], both[1])
                )
                cols = slice(g * 128, g * 128 + 128)
                mixed[at, cols] = (attention + weight * (swept + 2.0 * qrows[at, cols])).astype(B)

    def part(d):
        cols = pl.ds(pl.multiple_of(d * WIDTH, WIDTH), WIDTH)
        return mm(mixed[...], w[:, cols])

    def parcel(k):
        return pltpu.make_async_remote_copy(
            src_ref=terms.at[k],
            dst_ref=got.at[me],
            send_sem=send_sem.at[k],
            recv_sem=recv_sem.at[me],
            device_id={"head": lax.rem(me + k, N_HEAD)},
            device_id_type=MESH,
        )

    @pl.loop(1, N_HEAD)
    def _(k):
        terms[k] = part(lax.rem(me + k, N_HEAD)).astype(B)
        parcel(k).start()

    def gather(k, total):
        s = lax.rem(me + N_HEAD - k, N_HEAD)
        pltpu.make_async_copy(got.at[s], got.at[s], recv_sem.at[s]).wait()
        return total + got[s].astype(F)

    out[...] = lax.fori_loop(1, N_HEAD, gather, part(me)).astype(B)
    pl.loop(1, N_HEAD)(lambda k: parcel(k).wait_send())


def local(
    tokens,
    qkv_weight,
    out_weight,
    segment_ids,
    inner_w1,
    inner_b1,
    inner_w2,
    inner_b2,
    norm_gain,
    norm_bias,
    inner_rate,
    out_gate,
):
    rows = tokens.shape[0]
    dma = pltpu.SemaphoreType.DMA
    vm, sm, hbm = (pl.BlockSpec(memory_space=m) for m in (pltpu.VMEM, pltpu.SMEM, pl.ANY))
    return pl.pallas_call(
        layer_kernel,
        out_shape=jax.ShapeDtypeStruct((rows, WIDTH), B),
        in_specs=[vm, hbm, hbm, sm, sm] + [vm] * 7,
        out_specs=vm,
        scratch_shapes=[
            pltpu.VMEM((N_HEAD, rows, WIDTH), B),
            pltpu.VMEM(qkv_weight.shape, B),
            pltpu.VMEM((rows, 3 * WIDTH), F),
            pltpu.VMEM((2 * HEADS, PACK, 128), B),
            pltpu.VMEM((rows, WIDTH), F),
            pltpu.VMEM(out_weight.shape, B),
            pltpu.VMEM((N_TM, PACK, 128), B),
            pltpu.VMEM((N_TM, 128, 128), B),
            pltpu.VMEM((UNITS, 256, 128), F),
            pltpu.VMEM((128, 256), F),
            pltpu.VMEM((64, 256), F),
            pltpu.VMEM((64, 256), B),
            pltpu.VMEM((1, 128), F),
            pltpu.VMEM((3 * HEADS, 128, 128), B),
            pltpu.VMEM((rows, WIDTH), B),
            pltpu.VMEM((N_HEAD, rows, WIDTH), B),
            pltpu.VMEM((N_HEAD, rows, WIDTH), B),
            dma((9,)),
            dma((N_HEAD, 2)),
            dma,
            dma,
            dma((PLACES,)),
            dma((N_TM,)),
            dma,
            dma((N_TM,)),
            dma((N_TM,)),
            dma((3 * HEADS,)),
            dma((N_HEAD,)),
            dma((N_HEAD,)),
        ],
        compiler_params=pltpu.CompilerParams(
            collective_id=1, has_side_effects=True, vmem_limit_bytes=56 * 2**20
        ),
        name="layer",
    )(
        tokens,
        qkv_weight,
        out_weight,
        inner_rate,
        segment_ids,
        inner_w1,
        inner_b1,
        jnp.swapaxes(inner_w2, 1, 2),
        inner_b2,
        norm_gain,
        norm_bias,
        out_gate,
    )


def solution(mesh):
    placed = (
        P("tm", "head"),
        P(None, None, "head"),
        P("head", None),
        P(),
        P("head", None, None),
        P("head", None),
        P("head", None, None),
        P("head", None),
        P("head", None),
        P("head", None),
        P("head"),
        P("head", None),
    )
    return jax.shard_map(
        local, mesh=mesh, in_specs=placed, out_specs=P("tm", "head"), check_vma=False
    )
```

```python
import jax
import jax.numpy as jnp
from jax import lax
from jax.experimental import pallas as pl
from jax.experimental.pallas import tpu as pltpu
from jax.sharding import PartitionSpec as P

MESH = pl.DeviceIdType.MESH
F = jnp.float32
B = jnp.bfloat16
HDIM = 64
GROUP = 64
EPS = 1e-06
NN = (((1,), (0,)), ((), ()))
NT = (((1,), (1,)), ((), ()))
TN = (((0,), (0,)), ((), ()))
C0 = 0.7978845608028654
C1 = 0.044715
N_TM = 32
HEADS = 6
BLOCKS = 128
PACK = 384
CHAINS = 2 * HEADS
PLACES = 2 * HEADS
HALF = N_TM // 2
WINDOW = 4096 // 256 + 1
UNITS = HALF + 2
FAR = 1 << 20
N_HEAD = 8
WIDTH = HEADS * HDIM


def mm(a, b, dims=NN):
    return lax.dot_general(a, b, dims, preferred_element_type=F)


def gelu_both(x):
    x2 = x * x
    th = jnp.tanh(x * (C0 + (C0 * C1) * x2))
    hp = 0.5 + 0.5 * th
    return x * hp, hp + (hp - hp * hp) * (x * (2 * C0 + (6 * C0 * C1) * x2))


def gelu(x):
    x2 = x * x
    th = jnp.tanh(x * (C0 + (C0 * C1) * x2))
    return x * (0.5 + 0.5 * th)


def mean(x):
    return jnp.mean(x, -1, keepdims=True)


def lanes(shape):
    return lax.broadcasted_iota(jnp.int32, shape, 1)


def chain(rev, rate, buf, w1, b1, w2, b2i, gn, bs, out, W1, W2, W2b, b2, arrived, finished):
    g2 = gn * gn
    s = rate / (GROUP * HDIM)
    lane = lanes((64, 128))
    tail = jnp.where(lane == 64, 1.0, 0.0).astype(B)

    def place(step):
        b = jnp.clip(step, 0, BLOCKS - 1)
        b = jnp.where(rev, BLOCKS - 1 - b, b)
        return b // 4, b % 4

    def load_ka(step):
        i, j = place(step)
        return buf[i, pl.ds(pl.multiple_of(j * 64, 64), 64), :]

    def load_q(step):
        i, j = place(step)
        both = buf[i, pl.ds(pl.multiple_of(256 + (j // 2) * 64, 64), 64), :]
        swapped = jnp.concatenate([both[:, 64:], both[:, :64]], 1)
        return jnp.where(lane < 64, jnp.where(j % 2 == 0, both, swapped), tail)

    def augment(ka):
        return jnp.where(lane < 64, ka, tail)

    arrived(0)
    W1[0:64] = w1
    W1[64:128] = jnp.where(lax.broadcasted_iota(jnp.int32, (64, 256), 0) == 0, b1, 0.0)
    W2[...] = w2 - jnp.mean(w2, 0, keepdims=True)
    W2b[...] = W2[...].astype(B)
    valid = lane < 64
    valid_row = lanes((1, 128)) < 64

    def widen(x):
        return jnp.concatenate([x, jnp.zeros_like(x)], 1)

    def swap(x):
        return jnp.concatenate([x[:, 64:], x[:, :64]], 1)

    def rowsum(x):
        return jnp.sum(x, -1, keepdims=True) * (1.0 / HDIM)

    b2[...] = widen(b2i - mean(b2i))
    gn, bs, g2 = widen(gn), widen(bs), widen(g2)
    first = augment(load_ka(0))
    base0 = mm(first, W1[...].astype(B))
    zero_rows = jnp.zeros((64, 256), B)

    def body(t, carry):
        G1, base, Pt, KTs, Kt, Zlast = carry
        Ab = jnp.where(valid, swap(load_ka(t)), jnp.zeros((64, 128), B))
        A = Ab.astype(F)
        W2t = W2b[...]
        W2z = jnp.concatenate([W2t, zero_rows], 0)
        b2t = b2[...]
        R = mm(jnp.concatenate([Pt, KTs], 0), G1)
        Z1 = base - R[:64]
        W1n = W1[...] - R[64:]
        W1[...] = W1n
        W1b = W1n.astype(B)
        Kn = augment(load_ka(t + 1))
        Y = mm(jnp.concatenate([load_q(t - 1), Kn], 0), W1b)
        Zq = mm(gelu(Y[:64]).astype(B), W2z, NT) + b2t
        X2, dX = gelu_both(Z1)
        X2b = X2.astype(B)
        Z = mm(X2b, W2z, NT) + b2t
        Zg = Z * g2
        S1, S3, S4 = rowsum(Z * Z), rowsum(Z * Zg), rowsum(A * Z)
        inv = lax.rsqrt(S1 + EPS)
        a1 = inv * inv
        a3 = a1 * (a1 * S3 + inv * S4)
        G2 = a1 * Zg + inv * A - a3 * Z
        G2b = G2.astype(B)[:, :64]
        G1n = (mm(G2b, W2t) * dX).astype(B)
        U = mm(G2b, X2b, TN)
        W2n = W2[...] - s * U
        W2n = W2n - jnp.mean(W2n, 0, keepdims=True)
        W2b[...] = W2n.astype(B)
        W2[...] = W2n
        b2n = jnp.where(valid_row, b2t - s * jnp.sum(G2, 0, keepdims=True), 0.0)
        b2[...] = jnp.where(valid_row, b2n - rowsum(b2n), 0.0)
        Pn = (s * mm(Kn, Kt, NT)).astype(B)
        KTn = (s * Kt.astype(F)).T.astype(B)
        z = jnp.where(valid, Zlast - rowsum(Zlast), 0.0)
        o = (z * lax.rsqrt(rowsum(z * z) + EPS) * gn + bs).astype(B)
        i, j = place(t - 2)
        rows = pl.ds(pl.multiple_of((j // 2) * 64, 64), 64)
        out[i, rows, :] = jnp.where(valid == (j % 2 == 0), jnp.where(j % 2 == 0, o, swap(o)), out[i, rows, :])
        return G1n, Y[64:], Pn, KTn, Kn, Zq

    def group(i, carry):
        @pl.when(i + 1 < N_TM)
        def _():
            arrived(i + 1)

        carry = lax.fori_loop(4 * i, 4 * i + 4, body, carry)

        @pl.when(i > 0)
        def _():
            finished(i - 1)

        return carry

    carry = lax.fori_loop(
        0,
        N_TM,
        group,
        (
            jnp.zeros((64, 256), B),
            base0,
            jnp.zeros((64, 64), B),
            jnp.zeros((128, 64), B),
            first,
            jnp.zeros((64, 128), F),
        ),
    )
    lax.fori_loop(BLOCKS, BLOCKS + 2, body, carry)
    finished(N_TM - 1)


def first_at_least(ids, value):
    found = jnp.int32(0)
    for bit in range(13, -1, -1):
        trial = found + (1 << bit)
        last = ids[jnp.minimum(trial, N_TM * 256) - 1]
        found = jnp.where((trial <= N_TM * 256) & (last < value), trial, found)
    return found


def attend(half, ids, buf, parts, out, finished):
    c1, c2 = first_at_least(ids, 1), first_at_least(ids, 2)
    begin = half * HALF
    low = lanes((128, 128)) < 64
    row = lax.broadcasted_iota(jnp.int32, (256, 1), 0)
    inside = (row % 128) // 64 * 128 + (row // 128) * 64 + row % 64

    def segment(pos):
        return jnp.where(pos >= c1, 1, 0) + jnp.where(pos >= c2, 1, 0)

    def edge(number):
        return jnp.where(number <= 0, 0, jnp.where(number == 1, c1, jnp.where(number == 2, c2, FAR)))

    s0 = segment(begin * 256)
    next1, next2 = edge(s0 + 1) // 256, edge(s0 + 2) // 256

    def unit(u, _):
        above = jnp.where(begin + u - 1 >= next1, 1, 0) + jnp.where(begin + u - 2 >= next2, 1, 0)
        i = jnp.clip(begin + u - above, begin, begin + HALF - 1)
        left, right = edge(s0 + above), edge(s0 + above + 1)
        first = jnp.minimum(left // 256, N_TM - WINDOW)
        both = buf[i, 256:PACK, :]
        swapped = jnp.concatenate([both[:, 64:], both[:, :64]], 1)
        zero = jnp.zeros_like(both)
        q = jnp.concatenate([jnp.where(low, both, zero), jnp.where(low, swapped, zero)], 0)
        kv = buf[pl.ds(first, WINDOW), 0:256, :].reshape(WINDOW * 256, 128)
        pos = first * 256 + lanes((1, WINDOW * 256))
        scores = mm(q, kv, NT) + jnp.where((pos >= left) & (pos < right), 0.0, -1e30)
        w = jnp.exp(scores - jnp.max(scores, -1, keepdims=True))
        total = jnp.sum(w, -1, keepdims=True)
        parts[u] = mm(w.astype(B), kv) / total
        return 0

    lax.fori_loop(0, UNITS, unit, 0)

    def assemble(i, _):
        s1 = segment(i * 256)
        mine = segment(i * 256 + inside) - s1
        u = i - begin + s1 - s0
        o = jnp.where(
            mine == 0,
            parts[jnp.minimum(u, UNITS - 1)],
            jnp.where(
                mine == 1, parts[jnp.minimum(u + 1, UNITS - 1)], parts[jnp.minimum(u + 2, UNITS - 1)]
            ),
        )
        lo = jnp.concatenate([o[:128, 64:], o[:128, :64]], 1)
        out[i] = jnp.where(low, lo, o[128:]).astype(B)
        finished(i)
        return 0

    lax.fori_loop(begin, begin + HALF, assemble, 0)


def greet():
    barrier = pltpu.get_barrier_semaphore()
    for axis, n in (("head", N_HEAD), ("tm", N_TM)):
        me = lax.axis_index(axis)

        @pl.loop(1, n)
        def _(k):
            pl.semaphore_signal(
                barrier, inc=1, device_id={axis: lax.rem(me + k, n)}, device_id_type=MESH
            )

    pl.semaphore_wait(barrier, N_HEAD + N_TM - 2)


def device_of(place, core):
    y, m = place // 3, place % 3
    z = m + jnp.where(m >= y, 1, 0)
    return (y * 4 + z) * 2 + core


def slot_of(place):
    return place // 2 + HEADS * (place % 2)


def layer_kernel(
    tok, w_hbm, wo_hbm, rate, ids, w1, b1, w2, b2i, gain, bias, gate, final,
    toks, w, acc, src, qrows, wo, buf, out, parts, W1, W2, W2b, b2, res, mixed, terms, got,
    tok_send, tok_recv, w_sem, wo_sem, send_sem, recv_sem, own_sem, pass_sem, res_send, res_recv,
    term_send, term_recv,
):
    fetch = pltpu.make_async_copy(w_hbm, w, w_sem)
    fetch.start()
    fetch_out = pltpu.make_async_copy(wo_hbm, wo, wo_sem)
    fetch_out.start()
    greet()
    me = lax.axis_index("tm")
    core, y, z = me % 2, me // 8, me // 2 % 4
    place = y * 3 + z - jnp.where(z > y, 1, 0)
    active = y != z
    is_chain = active & (place % 2 == 0)
    is_attention = active & (place % 2 == 1)
    head = place // 2
    half = me // HALF
    short = pl.ds(0, 256)

    def parcel(r):
        return pltpu.make_async_remote_copy(
            src_ref=src.at[slot_of(r)],
            dst_ref=buf.at[me],
            send_sem=send_sem.at[r],
            recv_sem=recv_sem.at[me],
            device_id={"tm": device_of(r, half)},
            device_id_type=MESH,
        )

    def each(kind, count, act):
        @pl.loop(0, count)
        def _(k):
            r = 2 * k + kind

            @pl.when(device_of(r, half) != me)
            def _():
                act(r)

    def dispatch(kind, head_of):
        r = 2 * head_of + kind

        @pl.when(device_of(r, half) != me)
        def _():
            parcel(r).start()

    sent_tokens = project(
        tok, gain, bias, fetch, src, qrows, toks, w, acc, tok_send, tok_recv, dispatch
    )

    @pl.when(active & (core == half))
    def _():
        own = pltpu.make_async_copy(src.at[slot_of(place)], buf.at[me], own_sem)
        own.start()
        own.wait()

    def passing(i, part):
        block = buf.at[i, short] if part else buf.at[i]
        return pltpu.make_async_remote_copy(
            src_ref=block,
            dst_ref=block,
            send_sem=pass_sem.at[i],
            recv_sem=recv_sem.at[i],
            device_id={"tm": me + 1 - 2 * core},
            device_id_type=MESH,
        )

    def landed(i, part):
        direct = i // HALF == core

        @pl.when(direct & (i != me))
        def _():
            pltpu.make_async_copy(buf.at[i], buf.at[i], recv_sem.at[i]).wait()

        @pl.when(direct)
        def _():
            passing(i, part).start()

        @pl.when(jnp.logical_not(direct))
        def _():
            passing(i, part).wait_recv()

    def result(i):
        slot = jnp.where(is_chain, 2 * head + core, CHAINS + head)
        return out.at[i], res.at[slot], res_send.at[i], res_recv.at[slot]

    def away(i):
        block, there, sent, got = result(i)
        return pltpu.make_async_remote_copy(
            src_ref=block,
            dst_ref=there,
            send_sem=sent,
            recv_sem=got,
            device_id={"tm": i},
            device_id_type=MESH,
        )

    def here(i):
        block, there, sent, _ = result(i)
        return pltpu.make_async_copy(block, there, sent)

    def deliver(i):
        @pl.when(i != me)
        def _():
            away(i).start()

        @pl.when(i == me)
        def _():
            here(i).start()

    def delivered(i):
        @pl.when(i != me)
        def _():
            away(i).wait_send()

        @pl.when(i == me)
        def _():
            here(i).wait()

    def passed(part):
        pl.loop(core * HALF, core * HALF + HALF)(lambda i: passing(i, part).wait_send())

    @pl.when(is_chain)
    def _():
        rev = core == 1
        row = pl.ds(head, 1)

        def real(i):
            return jnp.where(rev, N_TM - 1 - i, i)

        chain(
            rev, rate[head], buf, w1[head], b1[row, :], w2[head], b2i[row, :], gain[row, :], bias[row, :],
            out, W1, W2, W2b, b2, lambda i: landed(real(i), False), lambda i: deliver(real(i)),
        )
        passed(False)
        pl.loop(0, N_TM)(delivered)

    @pl.when(is_attention)
    def _():
        pl.loop(core * HALF, core * HALF + HALF)(lambda i: landed(i, True))
        other = (1 - core) * HALF
        pl.loop(other, other + HALF)(lambda i: landed(i, True))
        attend(core, ids, buf, parts, out, deliver)
        passed(True)
        pl.loop(core * HALF, core * HALF + HALF)(delivered)


    @pl.loop(0, 3 * HEADS)
    def _(slot):
        origin = jnp.where(
            slot < CHAINS,
            device_of(slot // 2 * 2, slot % 2),
            device_of((slot - CHAINS) * 2 + 1, half),
        )

        @pl.when(origin != me)
        def _():
            pltpu.make_async_copy(res.at[slot], res.at[slot], res_recv.at[slot]).wait()

    fetch_out.wait()
    finish(res, qrows, gate, wo, final, mixed, terms, got, term_send, term_recv)
    each(0, HEADS, lambda r: parcel(r).wait_send())
    each(1, HEADS, lambda r: parcel(r).wait_send())
    sent_tokens()


def tile_row(ref, g):
    return jnp.concatenate([ref[2 * g : 2 * g + 1, :], ref[2 * g + 1 : 2 * g + 2, :]], 1)


def swap_halves(x):
    return jnp.concatenate([x[:, 64:], x[:, :64]], 1)


def project(tok, gain, bias, fetch, src, qrows, toks, w, acc, send_sem, recv_sem, dispatch):
    me = lax.axis_index("head")

    def add(x, s, fresh):
        rows = pl.ds(pl.multiple_of(s * WIDTH, WIDTH), WIDTH)
        for c in range(3):
            cols = slice(c * WIDTH, (c + 1) * WIDTH)
            y = mm(x, w[c, rows, :])
            acc[:, cols] = y if fresh else acc[:, cols] + y

    level, x = me // 4, me % 4

    def at(other, step):
        z = 1 - level if other else level
        return z * 4 + (x + step) % 4

    right, left, across = at(0, 1), at(0, 3), at(1, 0)
    sends = []

    def push(block, s, dest, part=None):
        rows = pl.ds(0, 256) if part is None else pl.ds(128 * part, 128)
        copy = pltpu.make_async_remote_copy(
            src_ref=block.at[rows],
            dst_ref=toks.at[s, rows],
            send_sem=send_sem.at[len(sends)],
            recv_sem=recv_sem.at[s, part or 0],
            device_id={"head": dest},
            device_id_type=MESH,
        )
        copy.start()
        sends.append(copy)

    def take(s, halves=False):
        for part in range(2 if halves else 1):
            rows = pl.ds(128 * part, 128) if halves else pl.ds(0, 256)
            piece = toks.at[s, rows]
            pltpu.make_async_copy(piece, piece, recv_sem.at[s, part]).wait()

    for dest in (across, right, left):
        push(tok, me, dest)
    fetch.wait()
    add(tok[...], me, True)
    take(across)
    push(toks.at[across], across, right)
    push(toks.at[across], across, left)
    for other in (0, 1):
        for step, dest, part in ((3, right, 0), (1, left, 1)):
            s = at(other, step)
            take(s)
            push(toks.at[s], s, dest, part)
            if not other and step == 3:
                add(toks[across], across, False)
            add(toks[s], s, False)
    for other in (0, 1):
        take(at(other, 2), True)
        add(toks[at(other, 2)], at(other, 2), False)

    low = lanes((256, 128)) < 64
    low_half = lanes((128, 128)) < 64
    r = lax.broadcasted_iota(jnp.int32, (128, 128), 0)
    same = jnp.where((r < 64) == low_half, 1.0 / HDIM, 0.0).astype(B)

    def group_mean(x):
        hi = x.astype(B)
        return mm(hi, same) + mm((x - hi.astype(F)).astype(B), same)

    def scaled(x):
        return x * lax.rsqrt(group_mean(x * x) + EPS)

    def pack_rows(left, right):
        pairs = [jnp.where(low, left, swap_halves(right)), jnp.where(low, swap_halves(left), right)]
        return pairs

    def pack_pairs(x):
        y = swap_halves(x)
        even = [jnp.where(low[:64], x[a : a + 64], y[a + 64 : a + 128]) for a in (0, 128)]
        odd = [jnp.where(low[:64], y[a : a + 64], x[a + 64 : a + 128]) for a in (0, 128)]
        return jnp.concatenate(even, 0), jnp.concatenate(odd, 0)

    def pack(g, left, right, quer, kind):
        tops, tails = pack_rows(left, right), pack_pairs(quer)
        for e in range(2):
            slot = HEADS * kind + 2 * g + e
            src[slot, 0:256, :] = tops[e].astype(B)
            src[slot, 256:PACK, :] = tails[e].astype(B)
            dispatch(kind, 2 * g + e)

    def raw(g):
        return (
            acc[:, c * WIDTH + g * 128 : c * WIDTH + (g + 1) * 128].astype(B).astype(F) for c in range(3)
        )

    for g in range(HEADS // 2):
        qn, kn, vn = (scaled(x) for x in raw(g))
        qrows[:, g * 128 : (g + 1) * 128] = qn
        aim = (tile_row(bias, g) - (vn - kn)) * tile_row(gain, g)
        pack(g, kn, aim - group_mean(aim), qn, 0)
    for g in range(HEADS // 2):
        q, k, v = raw(g)
        pack(g, k, v, q * HDIM**-0.5, 1)

    def sent():
        for copy in sends:
            copy.wait_send()

    return sent


def finish(res, qrows, gate, w, out, mixed, terms, got, send_sem, recv_sem):
    me = lax.axis_index("head")
    low = lanes((64, 128)) < 64
    for g in range(HEADS // 2):
        weight = jnp.tanh(tile_row(gate, g))
        for p in range(2):
            rows = slice(p * 64, p * 64 + 64)
            both = []
            for e in range(2):
                h = 2 * g + e
                swept = res[2 * h, rows, :].astype(F) + res[2 * h + 1, rows, :].astype(F)
                both.append((swept, res[CHAINS + h, rows, :].astype(F)))
            for c in range(2):
                at = slice((2 * p + c) * 64, (2 * p + c + 1) * 64)
                swept, attention = (
                    jnp.where(low, x, swap_halves(y)) if c == 0 else jnp.where(low, swap_halves(x), y)
                    for x, y in zip(both[0], both[1])
                )
                cols = slice(g * 128, g * 128 + 128)
                mixed[at, cols] = (attention + weight * (swept + 2.0 * qrows[at, cols])).astype(B)

    def part(d):
        cols = pl.ds(pl.multiple_of(d * WIDTH, WIDTH), WIDTH)
        return mm(mixed[...], w[:, cols])

    level, x = me // 4, me % 4

    def at(other, step):
        z = 1 - level if other else level
        return z * 4 + (x + step) % 4

    right, left, across = at(0, 1), at(0, 3), at(1, 0)
    first, second = pl.ds(0, 128), pl.ds(128, 128)
    sends = []

    def push(block, there, sem, dest):
        copy = pltpu.make_async_remote_copy(
            src_ref=block,
            dst_ref=there,
            send_sem=send_sem.at[len(sends)],
            recv_sem=recv_sem.at[sem],
            device_id={"head": dest},
            device_id_type=MESH,
        )
        copy.start()
        sends.append(copy)

    def take(block, sem):
        pltpu.make_async_copy(block, block, recv_sem.at[sem]).wait()

    for o in (1, 0):
        terms[o] = part(at(o, 2)).astype(B)
        push(terms.at[o, first], got.at[o, first], 2 * o, right)
        push(terms.at[o, second], got.at[o, second], 2 * o + 1, left)
    for o in (1, 0):
        mine = part(at(o, 1))
        take(got.at[o, first], 2 * o)
        terms[2 + o, 0:128] = (mine[:128] + got[o, 0:128].astype(F)).astype(B)
        terms[2 + o, 128:256] = mine[128:].astype(B)
        push(terms.at[2 + o], got.at[2 + o], 4 + 2 * o, right)
        mine = part(at(o, 3))
        take(got.at[o, second], 2 * o + 1)
        terms[4 + o, 0:128] = mine[:128].astype(B)
        terms[4 + o, 128:256] = (mine[128:] + got[o, 128:256].astype(F)).astype(B)
        push(terms.at[4 + o], got.at[4 + o], 5 + 2 * o, left)
    total = {}
    for o in (1, 0):
        mine = part(at(o, 0))
        take(got.at[2 + o], 4 + 2 * o)
        take(got.at[4 + o], 5 + 2 * o)
        total[o] = mine + got[2 + o].astype(F) + got[4 + o].astype(F)
        if o == 1:
            terms[6] = total[1].astype(B)
            push(terms.at[6], got.at[6], 8, across)
    take(got.at[6], 8)
    out[...] = (total[0] + got[6].astype(F)).astype(B)
    for copy in sends:
        copy.wait_send()


def local(
    tokens,
    qkv_weight,
    out_weight,
    segment_ids,
    inner_w1,
    inner_b1,
    inner_w2,
    inner_b2,
    norm_gain,
    norm_bias,
    inner_rate,
    out_gate,
):
    rows = tokens.shape[0]
    dma = pltpu.SemaphoreType.DMA
    vm, sm, hbm = (pl.BlockSpec(memory_space=m) for m in (pltpu.VMEM, pltpu.SMEM, pl.ANY))
    return pl.pallas_call(
        layer_kernel,
        out_shape=jax.ShapeDtypeStruct((rows, WIDTH), B),
        in_specs=[vm, hbm, hbm, sm, sm] + [vm] * 7,
        out_specs=vm,
        scratch_shapes=[
            pltpu.VMEM((N_HEAD, rows, WIDTH), B),
            pltpu.VMEM(qkv_weight.shape, B),
            pltpu.VMEM((rows, 3 * WIDTH), F),
            pltpu.VMEM((2 * HEADS, PACK, 128), B),
            pltpu.VMEM((rows, WIDTH), F),
            pltpu.VMEM(out_weight.shape, B),
            pltpu.VMEM((N_TM, PACK, 128), B),
            pltpu.VMEM((N_TM, 128, 128), B),
            pltpu.VMEM((UNITS, 256, 128), F),
            pltpu.VMEM((128, 256), F),
            pltpu.VMEM((64, 256), F),
            pltpu.VMEM((64, 256), B),
            pltpu.VMEM((1, 128), F),
            pltpu.VMEM((3 * HEADS, 128, 128), B),
            pltpu.VMEM((rows, WIDTH), B),
            pltpu.VMEM((N_HEAD, rows, WIDTH), B),
            pltpu.VMEM((N_HEAD, rows, WIDTH), B),
            dma((9,)),
            dma((N_HEAD, 2)),
            dma,
            dma,
            dma((PLACES,)),
            dma((N_TM,)),
            dma,
            dma((N_TM,)),
            dma((N_TM,)),
            dma((3 * HEADS,)),
            dma((9,)),
            dma((9,)),
        ],
        compiler_params=pltpu.CompilerParams(
            collective_id=1, has_side_effects=True, vmem_limit_bytes=56 * 2**20
        ),
        name="layer",
    )(
        tokens,
        qkv_weight,
        out_weight,
        inner_rate,
        segment_ids,
        inner_w1,
        inner_b1,
        jnp.swapaxes(inner_w2, 1, 2),
        inner_b2,
        norm_gain,
        norm_bias,
        out_gate,
    )


def solution(mesh):
    placed = (
        P("tm", "head"),
        P(None, None, "head"),
        P("head", None),
        P(),
        P("head", None, None),
        P("head", None),
        P("head", None, None),
        P("head", None),
        P("head", None),
        P("head", None),
        P("head"),
        P("head", None),
    )
    return jax.shard_map(
        local, mesh=mesh, in_specs=placed, out_specs=P("tm", "head"), check_vma=False
    )
```

```python
import jax
import jax.numpy as jnp
from jax import lax
from jax.experimental import pallas as pl
from jax.experimental.pallas import tpu as pltpu
from jax.sharding import PartitionSpec as P

MESH = pl.DeviceIdType.MESH
F = jnp.float32
B = jnp.bfloat16
HDIM = 64
GROUP = 64
EPS = 1e-06
NN = (((1,), (0,)), ((), ()))
NT = (((1,), (1,)), ((), ()))
TN = (((0,), (0,)), ((), ()))
C0 = 0.7978845608028654
C1 = 0.044715
N_TM = 32
HEADS = 6
BLOCKS = 128
PACK = 384
CHAINS = 2 * HEADS
PLACES = 2 * HEADS
HALF = N_TM // 2
WINDOW = 4096 // 256 + 1
UNITS = HALF + 2
FAR = 1 << 20
N_HEAD = 8
WIDTH = HEADS * HDIM


def mm(a, b, dims=NN):
    return lax.dot_general(a, b, dims, preferred_element_type=F)


def gelu_both(x):
    x2 = x * x
    th = jnp.tanh(x * (C0 + (C0 * C1) * x2))
    hp = 0.5 + 0.5 * th
    return x * hp, hp + (hp - hp * hp) * (x * (2 * C0 + (6 * C0 * C1) * x2))


def gelu(x):
    x2 = x * x
    th = jnp.tanh(x * (C0 + (C0 * C1) * x2))
    return x * (0.5 + 0.5 * th)


def mean(x):
    return jnp.mean(x, -1, keepdims=True)


def lanes(shape):
    return lax.broadcasted_iota(jnp.int32, shape, 1)


def chain(rev, rate, buf, w1, b1, w2, b2i, gn, bs, out, W1, W2, W2b, b2, arrived, finished):
    g2 = gn * gn
    s = rate / (GROUP * HDIM)
    lane = lanes((64, 128))
    tail = jnp.where(lane == 64, 1.0, 0.0).astype(B)

    def place(step):
        b = jnp.clip(step, 0, BLOCKS - 1)
        b = jnp.where(rev, BLOCKS - 1 - b, b)
        return b // 4, b % 4

    def load_ka(step):
        i, j = place(step)
        return buf[i, pl.ds(pl.multiple_of(j * 64, 64), 64), :]

    def load_q(step):
        i, j = place(step)
        both = buf[i, pl.ds(pl.multiple_of(256 + (j // 2) * 64, 64), 64), :]
        swapped = jnp.concatenate([both[:, 64:], both[:, :64]], 1)
        return jnp.where(lane < 64, jnp.where(j % 2 == 0, both, swapped), tail)

    def augment(ka):
        return jnp.where(lane < 64, ka, tail)

    arrived(0)
    W1[0:64] = w1
    W1[64:128] = jnp.where(lax.broadcasted_iota(jnp.int32, (64, 256), 0) == 0, b1, 0.0)
    W2[...] = w2 - jnp.mean(w2, 0, keepdims=True)
    W2b[...] = W2[...].astype(B)
    valid = lane < 64
    valid_row = lanes((1, 128)) < 64

    def widen(x):
        return jnp.concatenate([x, jnp.zeros_like(x)], 1)

    def swap(x):
        return jnp.concatenate([x[:, 64:], x[:, :64]], 1)

    def rowsum(x):
        return jnp.sum(x, -1, keepdims=True) * (1.0 / HDIM)

    b2[...] = widen(b2i - mean(b2i))
    gn, bs, g2 = widen(gn), widen(bs), widen(g2)
    first = augment(load_ka(0))
    base0 = mm(first, W1[...].astype(B))
    zero_rows = jnp.zeros((64, 256), B)

    def body(t, carry):
        G1, base, Pt, KTs, Kt, Zlast = carry
        Ab = jnp.where(valid, swap(load_ka(t)), jnp.zeros((64, 128), B))
        A = Ab.astype(F)
        W2t = W2b[...]
        W2z = jnp.concatenate([W2t, zero_rows], 0)
        b2t = b2[...]
        R = mm(jnp.concatenate([Pt, KTs], 0), G1)
        Z1 = base - R[:64]
        W1n = W1[...] - R[64:]
        W1[...] = W1n
        W1b = W1n.astype(B)
        Kn = augment(load_ka(t + 1))
        Y = mm(jnp.concatenate([load_q(t - 1), Kn], 0), W1b)
        Zq = mm(gelu(Y[:64]).astype(B), W2z, NT) + b2t
        X2, dX = gelu_both(Z1)
        X2b = X2.astype(B)
        Z = mm(X2b, W2z, NT) + b2t
        Zg = Z * g2
        S1, S3, S4 = rowsum(Z * Z), rowsum(Z * Zg), rowsum(A * Z)
        inv = lax.rsqrt(S1 + EPS)
        a1 = inv * inv
        a3 = a1 * (a1 * S3 + inv * S4)
        G2 = a1 * Zg + inv * A - a3 * Z
        G2b = G2.astype(B)[:, :64]
        G1n = (mm(G2b, W2t) * dX).astype(B)
        U = mm(G2b, X2b, TN)
        W2n = W2[...] - s * U
        W2n = W2n - jnp.mean(W2n, 0, keepdims=True)
        W2b[...] = W2n.astype(B)
        W2[...] = W2n
        b2n = jnp.where(valid_row, b2t - s * jnp.sum(G2, 0, keepdims=True), 0.0)
        b2[...] = jnp.where(valid_row, b2n - rowsum(b2n), 0.0)
        Pn = (s * mm(Kn, Kt, NT)).astype(B)
        KTn = (s * Kt.astype(F)).T.astype(B)
        z = jnp.where(valid, Zlast - rowsum(Zlast), 0.0)
        o = (z * lax.rsqrt(rowsum(z * z) + EPS) * gn + bs).astype(B)
        i, j = place(t - 2)
        rows = pl.ds(pl.multiple_of((j // 2) * 64, 64), 64)
        out[i, rows, :] = jnp.where(valid == (j % 2 == 0), jnp.where(j % 2 == 0, o, swap(o)), out[i, rows, :])
        return G1n, Y[64:], Pn, KTn, Kn, Zq

    def group(i, carry):
        @pl.when(i + 1 < N_TM)
        def _():
            arrived(i + 1)

        carry = lax.fori_loop(4 * i, 4 * i + 4, body, carry)

        @pl.when(i > 0)
        def _():
            finished(i - 1)

        return carry

    carry = lax.fori_loop(
        0,
        N_TM,
        group,
        (
            jnp.zeros((64, 256), B),
            base0,
            jnp.zeros((64, 64), B),
            jnp.zeros((128, 64), B),
            first,
            jnp.zeros((64, 128), F),
        ),
    )
    lax.fori_loop(BLOCKS, BLOCKS + 2, body, carry)
    finished(N_TM - 1)


def first_at_least(ids, value):
    found = jnp.int32(0)
    for bit in range(13, -1, -1):
        trial = found + (1 << bit)
        last = ids[jnp.minimum(trial, N_TM * 256) - 1]
        found = jnp.where((trial <= N_TM * 256) & (last < value), trial, found)
    return found


def attend(half, ids, buf, parts, out, finished):
    c1, c2 = first_at_least(ids, 1), first_at_least(ids, 2)
    begin = half * HALF
    low = lanes((128, 128)) < 64
    row = lax.broadcasted_iota(jnp.int32, (256, 1), 0)
    inside = (row % 128) // 64 * 128 + (row // 128) * 64 + row % 64

    def segment(pos):
        return jnp.where(pos >= c1, 1, 0) + jnp.where(pos >= c2, 1, 0)

    def edge(number):
        return jnp.where(number <= 0, 0, jnp.where(number == 1, c1, jnp.where(number == 2, c2, FAR)))

    s0 = segment(begin * 256)
    next1, next2 = edge(s0 + 1) // 256, edge(s0 + 2) // 256

    def unit(u, _):
        above = jnp.where(begin + u - 1 >= next1, 1, 0) + jnp.where(begin + u - 2 >= next2, 1, 0)
        i = jnp.clip(begin + u - above, begin, begin + HALF - 1)
        left, right = edge(s0 + above), edge(s0 + above + 1)
        first = jnp.minimum(left // 256, N_TM - WINDOW)
        both = buf[i, 256:PACK, :]
        swapped = jnp.concatenate([both[:, 64:], both[:, :64]], 1)
        zero = jnp.zeros_like(both)
        q = jnp.concatenate([jnp.where(low, both, zero), jnp.where(low, swapped, zero)], 0)
        kv = buf[pl.ds(first, WINDOW), 0:256, :].reshape(WINDOW * 256, 128)
        pos = first * 256 + lanes((1, WINDOW * 256))
        scores = mm(q, kv, NT) + jnp.where((pos >= left) & (pos < right), 0.0, -1e30)
        w = jnp.exp(scores - jnp.max(scores, -1, keepdims=True))
        total = jnp.sum(w, -1, keepdims=True)
        parts[u] = mm(w.astype(B), kv) / total
        return 0

    lax.fori_loop(0, UNITS, unit, 0)

    def assemble(i, _):
        s1 = segment(i * 256)
        mine = segment(i * 256 + inside) - s1
        u = i - begin + s1 - s0
        o = jnp.where(
            mine == 0,
            parts[jnp.minimum(u, UNITS - 1)],
            jnp.where(
                mine == 1, parts[jnp.minimum(u + 1, UNITS - 1)], parts[jnp.minimum(u + 2, UNITS - 1)]
            ),
        )
        lo = jnp.concatenate([o[:128, 64:], o[:128, :64]], 1)
        out[i] = jnp.where(low, lo, o[128:]).astype(B)
        finished(i)
        return 0

    lax.fori_loop(begin, begin + HALF, assemble, 0)


def greet():
    barrier = pltpu.get_barrier_semaphore()
    for axis, n in (("head", N_HEAD), ("tm", N_TM)):
        me = lax.axis_index(axis)

        @pl.loop(1, n)
        def _(k):
            pl.semaphore_signal(
                barrier, inc=1, device_id={axis: lax.rem(me + k, n)}, device_id_type=MESH
            )

    pl.semaphore_wait(barrier, N_HEAD + N_TM - 2)


def device_of(place, core):
    y, m = place // 3, place % 3
    z = m + jnp.where(m >= y, 1, 0)
    return (y * 4 + z) * 2 + core


def slot_of(place):
    return place // 2 + HEADS * (place % 2)


def layer_kernel(
    tok, w_hbm, wo_hbm, rate, ids, w1, b1, w2, b2i, gain, bias, gate, final,
    toks, w, acc, src, qrows, wo, buf, out, parts, W1, W2, W2b, b2, res, mixed, terms, got,
    tok_send, tok_recv, w_sem, wo_sem, send_sem, recv_sem, own_sem, pass_sem, res_send, res_recv,
    term_send, term_recv,
):
    fetch = pltpu.make_async_copy(w_hbm, w, w_sem)
    fetch.start()
    fetch_out = pltpu.make_async_copy(wo_hbm, wo, wo_sem)
    fetch_out.start()
    greet()
    me = lax.axis_index("tm")
    core, y, z = me % 2, me // 8, me // 2 % 4
    place = y * 3 + z - jnp.where(z > y, 1, 0)
    active = y != z
    is_chain = active & (place % 2 == 0)
    is_attention = active & (place % 2 == 1)
    head = place // 2
    half = me // HALF
    short = pl.ds(0, 256)

    def parcel(r):
        return pltpu.make_async_remote_copy(
            src_ref=src.at[slot_of(r)],
            dst_ref=buf.at[me],
            send_sem=send_sem.at[r],
            recv_sem=recv_sem.at[me],
            device_id={"tm": device_of(r, half)},
            device_id_type=MESH,
        )

    def each(kind, count, act):
        @pl.loop(0, count)
        def _(k):
            r = 2 * k + kind

            @pl.when(device_of(r, half) != me)
            def _():
                act(r)

    def dispatch(kind, head_of):
        r = 2 * head_of + kind

        @pl.when(device_of(r, half) != me)
        def _():
            parcel(r).start()

    sent_tokens = project(
        tok, gain, bias, fetch, src, qrows, toks, w, acc, tok_send, tok_recv, dispatch
    )

    @pl.when(active & (core == half))
    def _():
        own = pltpu.make_async_copy(src.at[slot_of(place)], buf.at[me], own_sem)
        own.start()
        own.wait()

    def passing(i, part):
        block = buf.at[i, short] if part else buf.at[i]
        return pltpu.make_async_remote_copy(
            src_ref=block,
            dst_ref=block,
            send_sem=pass_sem.at[i],
            recv_sem=recv_sem.at[i],
            device_id={"tm": me + 1 - 2 * core},
            device_id_type=MESH,
        )

    def landed(i, part):
        direct = i // HALF == core

        @pl.when(direct & (i != me))
        def _():
            pltpu.make_async_copy(buf.at[i], buf.at[i], recv_sem.at[i]).wait()

        @pl.when(direct)
        def _():
            passing(i, part).start()

        @pl.when(jnp.logical_not(direct))
        def _():
            passing(i, part).wait_recv()

    def result(i):
        slot = jnp.where(is_chain, 2 * head + core, CHAINS + head)
        return out.at[i], res.at[slot], res_send.at[i], res_recv.at[slot]

    def away(i):
        block, there, sent, got = result(i)
        return pltpu.make_async_remote_copy(
            src_ref=block,
            dst_ref=there,
            send_sem=sent,
            recv_sem=got,
            device_id={"tm": i},
            device_id_type=MESH,
        )

    def here(i):
        block, there, sent, _ = result(i)
        return pltpu.make_async_copy(block, there, sent)

    def deliver(i):
        @pl.when(i != me)
        def _():
            away(i).start()

        @pl.when(i == me)
        def _():
            here(i).start()

    def delivered(i):
        @pl.when(i != me)
        def _():
            away(i).wait_send()

        @pl.when(i == me)
        def _():
            here(i).wait()

    def passed(part):
        pl.loop(core * HALF, core * HALF + HALF)(lambda i: passing(i, part).wait_send())

    @pl.when(is_chain)
    def _():
        rev = core == 1
        row = pl.ds(head, 1)

        def real(i):
            return jnp.where(rev, N_TM - 1 - i, i)

        chain(
            rev, rate[head], buf, w1[head], b1[row, :], w2[head], b2i[row, :], gain[row, :], bias[row, :],
            out, W1, W2, W2b, b2, lambda i: landed(real(i), False), lambda i: deliver(real(i)),
        )
        passed(False)
        pl.loop(0, N_TM)(delivered)

    @pl.when(is_attention)
    def _():
        pl.loop(core * HALF, core * HALF + HALF)(lambda i: landed(i, True))
        other = (1 - core) * HALF
        pl.loop(other, other + HALF)(lambda i: landed(i, True))
        attend(core, ids, buf, parts, out, deliver)
        passed(True)
        pl.loop(core * HALF, core * HALF + HALF)(delivered)


    @pl.loop(0, 3 * HEADS)
    def _(slot):
        origin = jnp.where(
            slot < CHAINS,
            device_of(slot // 2 * 2, slot % 2),
            device_of((slot - CHAINS) * 2 + 1, half),
        )

        @pl.when(origin != me)
        def _():
            pltpu.make_async_copy(res.at[slot], res.at[slot], res_recv.at[slot]).wait()

    fetch_out.wait()
    finish(res, qrows, gate, wo, final, mixed, terms, got, term_send, term_recv)
    each(0, HEADS, lambda r: parcel(r).wait_send())
    each(1, HEADS, lambda r: parcel(r).wait_send())
    sent_tokens()


def tile_row(ref, g):
    return jnp.concatenate([ref[2 * g : 2 * g + 1, :], ref[2 * g + 1 : 2 * g + 2, :]], 1)


def swap_halves(x):
    return jnp.concatenate([x[:, 64:], x[:, :64]], 1)


def project(tok, gain, bias, fetch, src, qrows, toks, w, acc, send_sem, recv_sem, dispatch):
    me = lax.axis_index("head")

    def add(x, s, fresh):
        rows = pl.ds(pl.multiple_of(s * WIDTH, WIDTH), WIDTH)
        for c in range(3):
            cols = slice(c * WIDTH, (c + 1) * WIDTH)
            y = mm(x, w[c, rows, :])
            acc[:, cols] = y if fresh else acc[:, cols] + y

    level, x = me // 4, me % 4

    def at(other, step):
        z = 1 - level if other else level
        return z * 4 + (x + step) % 4

    right, left, across = at(0, 1), at(0, 3), at(1, 0)
    sends = []

    def push(block, s, dest, part=None):
        rows = pl.ds(0, 256) if part is None else pl.ds(128 * part, 128)
        copy = pltpu.make_async_remote_copy(
            src_ref=block.at[rows],
            dst_ref=toks.at[s, rows],
            send_sem=send_sem.at[len(sends)],
            recv_sem=recv_sem.at[s, part or 0],
            device_id={"head": dest},
            device_id_type=MESH,
        )
        copy.start()
        sends.append(copy)

    def take(s, halves=False):
        for part in range(2 if halves else 1):
            rows = pl.ds(128 * part, 128) if halves else pl.ds(0, 256)
            piece = toks.at[s, rows]
            pltpu.make_async_copy(piece, piece, recv_sem.at[s, part]).wait()

    for dest in (across, right, left):
        push(tok, me, dest)
    fetch.wait()
    add(tok[...], me, True)
    take(across)
    push(toks.at[across], across, right)
    push(toks.at[across], across, left)
    for other in (0, 1):
        for step, dest, part in ((3, right, 0), (1, left, 1)):
            s = at(other, step)
            take(s)
            push(toks.at[s], s, dest, part)
        if not other:
            add(toks[across], across, False)
    for other in (0, 1):
        for step in (3, 1):
            add(toks[at(other, step)], at(other, step), False)
    for other in (0, 1):
        take(at(other, 2), True)
        add(toks[at(other, 2)], at(other, 2), False)

    low = lanes((256, 128)) < 64
    low_half = lanes((128, 128)) < 64
    r = lax.broadcasted_iota(jnp.int32, (128, 128), 0)
    same = jnp.where((r < 64) == low_half, 1.0 / HDIM, 0.0).astype(B)

    def group_mean(x):
        hi = x.astype(B)
        return mm(hi, same) + mm((x - hi.astype(F)).astype(B), same)

    def scaled(x):
        return x * lax.rsqrt(group_mean(x * x) + EPS)

    def pack_rows(left, right):
        pairs = [jnp.where(low, left, swap_halves(right)), jnp.where(low, swap_halves(left), right)]
        return pairs

    def pack_pairs(x):
        y = swap_halves(x)
        even = [jnp.where(low[:64], x[a : a + 64], y[a + 64 : a + 128]) for a in (0, 128)]
        odd = [jnp.where(low[:64], y[a : a + 64], x[a + 64 : a + 128]) for a in (0, 128)]
        return jnp.concatenate(even, 0), jnp.concatenate(odd, 0)

    def pack(g, left, right, quer, kind):
        tops, tails = pack_rows(left, right), pack_pairs(quer)
        for e in range(2):
            slot = HEADS * kind + 2 * g + e
            src[slot, 0:256, :] = tops[e].astype(B)
            src[slot, 256:PACK, :] = tails[e].astype(B)
            dispatch(kind, 2 * g + e)

    def raw(g):
        return (
            acc[:, c * WIDTH + g * 128 : c * WIDTH + (g + 1) * 128].astype(B).astype(F) for c in range(3)
        )

    for g in range(HEADS // 2):
        qn, kn, vn = (scaled(x) for x in raw(g))
        qrows[:, g * 128 : (g + 1) * 128] = qn
        aim = (tile_row(bias, g) - (vn - kn)) * tile_row(gain, g)
        pack(g, kn, aim - group_mean(aim), qn, 0)
    for g in range(HEADS // 2):
        q, k, v = raw(g)
        pack(g, k, v, q * HDIM**-0.5, 1)

    def sent():
        for copy in sends:
            copy.wait_send()

    return sent


def finish(res, qrows, gate, w, out, mixed, terms, got, send_sem, recv_sem):
    me = lax.axis_index("head")
    low = lanes((64, 128)) < 64
    for g in range(HEADS // 2):
        weight = jnp.tanh(tile_row(gate, g))
        for p in range(2):
            rows = slice(p * 64, p * 64 + 64)
            both = []
            for e in range(2):
                h = 2 * g + e
                swept = res[2 * h, rows, :].astype(F) + res[2 * h + 1, rows, :].astype(F)
                both.append((swept, res[CHAINS + h, rows, :].astype(F)))
            for c in range(2):
                at = slice((2 * p + c) * 64, (2 * p + c + 1) * 64)
                swept, attention = (
                    jnp.where(low, x, swap_halves(y)) if c == 0 else jnp.where(low, swap_halves(x), y)
                    for x, y in zip(both[0], both[1])
                )
                cols = slice(g * 128, g * 128 + 128)
                mixed[at, cols] = (attention + weight * (swept + 2.0 * qrows[at, cols])).astype(B)

    def part(d):
        cols = pl.ds(pl.multiple_of(d * WIDTH, WIDTH), WIDTH)
        return mm(mixed[...], w[:, cols])

    level, x = me // 4, me % 4

    def at(other, step):
        z = 1 - level if other else level
        return z * 4 + (x + step) % 4

    right, left, across = at(0, 1), at(0, 3), at(1, 0)
    first, second = pl.ds(0, 128), pl.ds(128, 128)
    sends = []

    def push(block, there, sem, dest):
        copy = pltpu.make_async_remote_copy(
            src_ref=block,
            dst_ref=there,
            send_sem=send_sem.at[len(sends)],
            recv_sem=recv_sem.at[sem],
            device_id={"head": dest},
            device_id_type=MESH,
        )
        copy.start()
        sends.append(copy)

    def take(block, sem):
        pltpu.make_async_copy(block, block, recv_sem.at[sem]).wait()

    for o in (1, 0):
        terms[o] = part(at(o, 2)).astype(B)
        push(terms.at[o, first], got.at[o, first], 2 * o, right)
        push(terms.at[o, second], got.at[o, second], 2 * o + 1, left)
    for o in (1, 0):
        mine = part(at(o, 1))
        take(got.at[o, first], 2 * o)
        terms[2 + o, 0:128] = (mine[:128] + got[o, 0:128].astype(F)).astype(B)
        terms[2 + o, 128:256] = mine[128:].astype(B)
        push(terms.at[2 + o], got.at[2 + o], 4 + 2 * o, right)
        mine = part(at(o, 3))
        take(got.at[o, second], 2 * o + 1)
        terms[4 + o, 0:128] = mine[:128].astype(B)
        terms[4 + o, 128:256] = (mine[128:] + got[o, 128:256].astype(F)).astype(B)
        push(terms.at[4 + o], got.at[4 + o], 5 + 2 * o, left)
    total = {}
    for o in (1, 0):
        mine = part(at(o, 0))
        take(got.at[2 + o], 4 + 2 * o)
        take(got.at[4 + o], 5 + 2 * o)
        total[o] = mine + got[2 + o].astype(F) + got[4 + o].astype(F)
        if o == 1:
            terms[6] = total[1].astype(B)
            push(terms.at[6], got.at[6], 8, across)
    take(got.at[6], 8)
    out[...] = (total[0] + got[6].astype(F)).astype(B)
    for copy in sends:
        copy.wait_send()


def local(
    tokens,
    qkv_weight,
    out_weight,
    segment_ids,
    inner_w1,
    inner_b1,
    inner_w2,
    inner_b2,
    norm_gain,
    norm_bias,
    inner_rate,
    out_gate,
):
    rows = tokens.shape[0]
    dma = pltpu.SemaphoreType.DMA
    vm, sm, hbm = (pl.BlockSpec(memory_space=m) for m in (pltpu.VMEM, pltpu.SMEM, pl.ANY))
    return pl.pallas_call(
        layer_kernel,
        out_shape=jax.ShapeDtypeStruct((rows, WIDTH), B),
        in_specs=[vm, hbm, hbm, sm, sm] + [vm] * 7,
        out_specs=vm,
        scratch_shapes=[
            pltpu.VMEM((N_HEAD, rows, WIDTH), B),
            pltpu.VMEM(qkv_weight.shape, B),
            pltpu.VMEM((rows, 3 * WIDTH), F),
            pltpu.VMEM((2 * HEADS, PACK, 128), B),
            pltpu.VMEM((rows, WIDTH), F),
            pltpu.VMEM(out_weight.shape, B),
            pltpu.VMEM((N_TM, PACK, 128), B),
            pltpu.VMEM((N_TM, 128, 128), B),
            pltpu.VMEM((UNITS, 256, 128), F),
            pltpu.VMEM((128, 256), F),
            pltpu.VMEM((64, 256), F),
            pltpu.VMEM((64, 256), B),
            pltpu.VMEM((1, 128), F),
            pltpu.VMEM((3 * HEADS, 128, 128), B),
            pltpu.VMEM((rows, WIDTH), B),
            pltpu.VMEM((N_HEAD, rows, WIDTH), B),
            pltpu.VMEM((N_HEAD, rows, WIDTH), B),
            dma((9,)),
            dma((N_HEAD, 2)),
            dma,
            dma,
            dma((PLACES,)),
            dma((N_TM,)),
            dma,
            dma((N_TM,)),
            dma((N_TM,)),
            dma((3 * HEADS,)),
            dma((9,)),
            dma((9,)),
        ],
        compiler_params=pltpu.CompilerParams(
            collective_id=1, has_side_effects=True, vmem_limit_bytes=56 * 2**20
        ),
        name="layer",
    )(
        tokens,
        qkv_weight,
        out_weight,
        inner_rate,
        segment_ids,
        inner_w1,
        inner_b1,
        jnp.swapaxes(inner_w2, 1, 2),
        inner_b2,
        norm_gain,
        norm_bias,
        out_gate,
    )


def solution(mesh):
    placed = (
        P("tm", "head"),
        P(None, None, "head"),
        P("head", None),
        P(),
        P("head", None, None),
        P("head", None),
        P("head", None, None),
        P("head", None),
        P("head", None),
        P("head", None),
        P("head"),
        P("head", None),
    )
    return jax.shard_map(
        local, mesh=mesh, in_specs=placed, out_specs=P("tm", "head"), check_vma=False
    )
```
